32 devices in a mesh: loop: 4 (over z), rep: 4 (over y, x), sec: 2 (over core).
Axes of the slice: x: 2, y: 2, z: 4, core: 2. Of those that a mesh axis runs over, the one named last changes fastest.
Arguments:
- student: bfloat16 [3072, 1024], P(('loop', 'rep'), 'sec'), may hold values from -6 to 6
- teacher: bfloat16 [3072, 4096], P(('loop', 'rep'), 'sec'), may hold values from -6 to 6
Outputs:
- student_grad: float32 [3072, 1024], P(('loop', 'rep'), 'sec')
The draws below stay inside these ranges and needn't reach their ends.
All inputs are finite; a program needn't handle non-finite values.
Results may differ from the reference program's by a relative error of at most 0.022.
Values may be sent and summed in bfloat16 or wider, within the bound.
A program may use at most 128 MiB of HBM per device.

```python
import math
import jax
import jax.numpy as jnp
from jax import lax

DS = 1024
DT = 4096
BLOCK = 768
PASSAGES = 3072
N_LOOP = 4


def shard_levels(own_key, shape, pieces, smallest, top_value):
    gain = 1.0
    for dim, shards_of in pieces:
        draws = jax.random.uniform(jax.random.fold_in(jax.random.fold_in(own_key, 6), dim), (shards_of,), jnp.float32, smallest / len(pieces), top_value / len(pieces))
        gain = gain * jnp.repeat(jnp.exp(draws), shape[dim] // shards_of).reshape((-1,) + (1,) * (len(shape) - 1 - dim))
    return gain


def gaussian(rng, extent, spread, reach, cuts=(), held_as=jnp.bfloat16):
    gain = shard_levels(rng, extent, cuts, -0.22, 0.18) if cuts else 1.0
    array = jax.random.normal(rng, extent, jnp.float32) * spread * gain
    return jnp.minimum(jnp.maximum(array, -reach), reach).astype(held_as)


def setup_inputs(seed: int = 0) -> dict:
    splits = jax.random.split(jax.random.key(seed), 3)
    student = gaussian(splits[0], (PASSAGES, DS), 1.0, 6.0, ((0, 16), (1, 2)))
    teacher = gaussian(splits[1], (PASSAGES, DT), 1.0, 6.0, ((0, 16), (1, 2)))
    return {"student": student, "teacher": teacher}


def reference(student, teacher):
    eps = 1e-06
    s32 = student.astype(jnp.float32)
    t32 = teacher.astype(jnp.float32)
    ssq_s = lax.optimization_barrier(jnp.sum(s32 * s32, axis=1)) + eps
    ssq_t = lax.optimization_barrier(jnp.sum(t32 * t32, axis=1)) + eps
    inv_s = lax.rsqrt(ssq_s)
    norm_s = (s32 * inv_s[:, None]).astype(jnp.bfloat16)
    norm_t = (t32 * lax.rsqrt(ssq_t)[:, None]).astype(jnp.bfloat16)
    coef = 32.0 * DS / math.sqrt(PASSAGES)
    blocks_s = norm_s.reshape(N_LOOP, BLOCK, DS)
    blocks_t = norm_t.reshape(N_LOOP, BLOCK, DT)

    def one_block(pair):
        rows_s, rows_t = pair
        first = jnp.dot(rows_s, norm_s.T, preferred_element_type=jnp.float32)
        second = jnp.dot(rows_t, norm_t.T, preferred_element_type=jnp.float32)
        mismatch = (first - second).astype(jnp.bfloat16)
        return coef * jnp.dot(mismatch, norm_s, preferred_element_type=jnp.float32)
    grad_n = lax.map(one_block, (blocks_s, blocks_t)).reshape(PASSAGES, DS)
    norm_f = norm_s.astype(jnp.float32)
    inner = lax.optimization_barrier(jnp.sum(grad_n * norm_f, axis=1))
    return (grad_n - inner[:, None] * norm_f) * inv_s[:, None]
```

```python
import functools
import math

import jax
import jax.numpy as jnp
from jax import lax
from jax.experimental import pallas as pl
from jax.experimental.pallas import tpu as pltpu
from jax.sharding import PartitionSpec as P

MESH = pl.DeviceIdType.MESH
LANES = 128
PIECE = 256
LAG = 2
EPS = 1e-6


def kernel(
    loops, reps, coef, dup, s_ref, t_ref, out_ref,
    stat_tx, stat_rx, inv_keep, cols_all, feats, feats_tx, own, right_tx, left_tx,
    from_left, from_right, full, part_tx, part_rx, part_own, inner_tx, inner_rx,
    stat_sem, gather_send, gather_recv, swap_send, swap_recv,
    right_send, right_recv, left_send, left_recv, part_send, part_recv, inner_sem,
):
    z = lax.axis_index("loop")
    b = lax.axis_index("rep")
    c = lax.axis_index("sec")
    rows, width = s_ref.shape
    pieces, total_rows, _ = feats.shape
    t_own = (pieces - 1) // 2
    strips = width // LANES
    steps = strips * pieces
    sibling = (z, b, 1 - c)
    has_left = z > 0
    has_right = z < loops - 1

    def peer(d):
        return lax.rem(b + d, reps)

    def span(q):
        return pl.ds(pl.multiple_of(q * rows, rows), rows)

    barrier = pltpu.get_barrier_semaphore()
    for d in range(1, reps):
        pl.semaphore_signal(barrier, inc=1, device_id=(z, peer(d), c), device_id_type=MESH)
    pl.semaphore_signal(barrier, inc=1, device_id=sibling, device_id_type=MESH)

    @pl.when(has_left)
    def _():
        pl.semaphore_signal(barrier, inc=1, device_id=(z - 1, b, c), device_id_type=MESH)

    @pl.when(has_right)
    def _():
        pl.semaphore_signal(barrier, inc=1, device_id=(z + 1, b, c), device_id_type=MESH)

    s32 = s_ref[...].astype(jnp.float32)
    t32 = t_ref[...].astype(jnp.float32)
    part_s = jnp.sum(s32 * s32, axis=1, keepdims=True)
    part_t = jnp.sum(t32 * t32, axis=1, keepdims=True)
    lane = lax.broadcasted_iota(jnp.int32, (rows, LANES), 1)
    stat_tx[...] = jnp.where(lane < LANES // 2, part_s, part_t)

    pl.semaphore_wait(barrier, reps + has_left.astype(jnp.int32) + has_right.astype(jnp.int32))

    def remote(src, dst, send, recv, device):
        return pltpu.make_async_remote_copy(
            src_ref=src, dst_ref=dst, send_sem=send, recv_sem=recv,
            device_id=device, device_id_type=MESH,
        )

    stat = remote(stat_tx, stat_rx, stat_sem.at[0], stat_sem.at[1], sibling)
    stat.start()
    stat.wait()
    inv = lax.rsqrt(stat_tx[...] + stat_rx[...] + EPS)
    inv_s = inv[:, :1]
    inv_t = inv[:, LANES - 1:]
    inv_keep[...] = jnp.broadcast_to(inv_s, (rows, LANES))
    mine = span(b)
    cols_all[mine, :] = (s_ref[...].astype(jnp.float32) * inv_s).astype(jnp.bfloat16)

    def to_peer(d, kind):
        q = peer(d)
        if kind == 0:
            return remote(cols_all.at[mine], cols_all.at[mine],
                          gather_send.at[0, d], gather_recv.at[0, d], (z, q, c))
        return remote(feats_tx.at[q], feats.at[pl.ds(1, t_own), mine],
                      gather_send.at[1, d], gather_recv.at[1, d], (z, q, c))

    for d in range(1, reps):
        to_peer(d, 0).start()
    for q in range(reps):
        for p in range(t_own):
            lo = (q * t_own + p) * PIECE
            feats_tx[q, p] = (t_ref[:, lo:lo + PIECE].astype(jnp.float32) * inv_t).astype(jnp.bfloat16)
    for d in range(1, reps):
        to_peer(d, 1).start()
    for p in range(t_own):
        feats[1 + p, mine, :] = feats_tx[b, p]

    block = pl.ds(pl.multiple_of((b // dup) * LANES, LANES), LANES)

    def to_sibling(d, kind):
        at = span(lax.rem(b - d + reps, reps))
        if kind == 0:
            return remote(cols_all.at[at, block], feats.at[0, at, pl.ds(LANES, LANES)],
                          swap_send.at[0, d], swap_recv.at[0, d], sibling)
        return remote(feats.at[pl.ds(1, t_own), at], feats.at[pl.ds(1 + t_own, t_own), at],
                      swap_send.at[1, d], swap_recv.at[1, d], sibling)

    for kind in (0, 1):
        for d in range(reps):
            if d:
                to_peer(d, kind).wait_recv()
            to_sibling(d, kind).start()
    feats[0, :, :LANES] = cols_all[:, block]

    def product(p):
        value = lax.dot_general(
            feats[p], cols_all[...], (((0,), (0,)), ((), ())), preferred_element_type=jnp.float32
        )
        for j in range(strips):
            own[j * pieces + p] = value[:, j * LANES:(j + 1) * LANES]

    for p in range(1, 1 + t_own):
        product(p)
    for kind in (0, 1):
        for d in range(reps):
            to_sibling(d, kind).wait_recv()
    product(0)
    for p in range(1 + t_own, pieces):
        product(p)

    def rightward(k):
        return remote(right_tx.at[k], from_left.at[k], right_send.at[k], right_recv.at[k], (z + 1, b, c))

    def leftward(k):
        return remote(left_tx.at[k], from_right.at[k], left_send.at[k], left_recv.at[k], (z - 1, b, c))

    def result(j, d):
        return remote(part_tx.at[j, peer(d)], part_rx.at[j, d],
                      part_send.at[j, d], part_recv.at[j, d], (z, peer(d), c))

    def up(k):
        @pl.when(has_left)
        def _():
            rightward(k).wait_recv()

        @pl.when(has_right)
        def _():
            @pl.when(has_left)
            def _():
                right_tx[k] = (own[k] + from_left[k].astype(jnp.float32)).astype(jnp.bfloat16)

            @pl.when(jnp.logical_not(has_left))
            def _():
                right_tx[k] = own[k].astype(jnp.bfloat16)
            rightward(k).start()

    def down(k):
        @pl.when(has_right)
        def _():
            leftward(k).wait_recv()

        @pl.when(has_left)
        def _():
            @pl.when(has_right)
            def _():
                left_tx[k] = (own[k] + from_right[k].astype(jnp.float32)).astype(jnp.bfloat16)

            @pl.when(jnp.logical_not(has_right))
            def _():
                left_tx[k] = own[k].astype(jnp.bfloat16)
            leftward(k).start()

    def finish(k):
        j = k // pieces
        p = lax.rem(k, pieces)

        @pl.when(has_left)
        def _():
            own[k] = own[k] + from_left[k].astype(jnp.float32)

        @pl.when(has_right)
        def _():
            own[k] = own[k] + from_right[k].astype(jnp.float32)
        full[p] = own[k].astype(jnp.bfloat16)

        @pl.when(p == pieces - 1)
        def _():
            value = jnp.dot(feats[0], full[0], preferred_element_type=jnp.float32)
            if dup > 1:
                value = value * (1.0 / dup)
            for q in range(1, pieces):
                value = value - jnp.dot(feats[q], full[q], preferred_element_type=jnp.float32)
            for q in range(reps):
                part_tx[j, q] = value[q * rows:(q + 1) * rows].astype(jnp.bfloat16)

                @pl.when(b == q)
                def _():
                    part_own[j] = value[q * rows:(q + 1) * rows]
            for d in range(1, reps):
                result(j, d).start()

    lag_up = LAG * z
    lag_down = LAG * (loops - 1 - z)
    lag_end = jnp.maximum(lag_up, lag_down)

    def step(i, carry):
        for lag, act in ((lag_up, up), (lag_down, down), (lag_end, finish)):
            k = i - lag

            @pl.when(jnp.logical_and(k >= 0, k < steps))
            def _():
                act(k)
        return carry

    lax.fori_loop(0, steps + LAG * (loops - 1), step, 0)

    norm = cols_all[mine, :].astype(jnp.float32)
    inner = jnp.zeros((rows, 1), jnp.float32)
    grads = []
    for j in range(strips):
        grad = part_own[j]
        for d in range(1, reps):
            result(j, d).wait_recv()
            grad = grad + part_rx[j, d].astype(jnp.float32)
        grad = grad * coef
        grads.append(grad)
        inner = inner + jnp.sum(grad * norm[:, j * LANES:(j + 1) * LANES], axis=1, keepdims=True)
    inner_tx[...] = jnp.broadcast_to(inner, (rows, LANES))
    swap = remote(inner_tx, inner_rx, inner_sem.at[0], inner_sem.at[1], sibling)
    swap.start()
    swap.wait_recv()
    inner_all = inner_tx[...] + inner_rx[...]
    for j in range(strips):
        at = slice(j * LANES, (j + 1) * LANES)
        out_ref[:, at] = (grads[j] - inner_all * norm[:, at]) * inv_keep[...]

    swap.wait_send()
    for kind in (0, 1):
        for d in range(reps):
            if d:
                to_peer(d, kind).wait_send()
            to_sibling(d, kind).wait_send()
    for j in range(strips):
        for d in range(1, reps):
            result(j, d).wait_send()

    def drain(k, carry):
        @pl.when(has_right)
        def _():
            rightward(k).wait_send()

        @pl.when(has_left)
        def _():
            leftward(k).wait_send()
        return carry

    lax.fori_loop(0, steps, drain, 0)


def body(loops, reps, student, teacher):
    rows, width = student.shape
    passages = rows * reps * loops
    coef = 32.0 * (2 * width) / math.sqrt(passages)
    dup = max(1, reps * LANES // width)
    t_own = teacher.shape[1] // (reps * PIECE)
    pieces = 1 + 2 * t_own
    strips = width // LANES
    steps = strips * pieces
    total = rows * reps
    f32, bf16 = jnp.float32, jnp.bfloat16
    dma = pltpu.SemaphoreType.DMA
    flops = 4 * total * pieces * PIECE * width
    return pl.pallas_call(
        functools.partial(kernel, loops, reps, coef, dup),
        out_shape=jax.ShapeDtypeStruct((rows, width), f32),
        in_specs=[pl.BlockSpec(memory_space=pltpu.VMEM)] * 2,
        out_specs=pl.BlockSpec(memory_space=pltpu.VMEM),
        scratch_shapes=[
            pltpu.VMEM((rows, LANES), f32),
            pltpu.VMEM((rows, LANES), f32),
            pltpu.VMEM((rows, LANES), f32),
            pltpu.VMEM((total, width), bf16),
            pltpu.VMEM((pieces, total, PIECE), bf16),
            pltpu.VMEM((reps, t_own, rows, PIECE), bf16),
            pltpu.VMEM((steps, PIECE, LANES), f32),
            pltpu.VMEM((steps, PIECE, LANES), bf16),
            pltpu.VMEM((steps, PIECE, LANES), bf16),
            pltpu.VMEM((steps, PIECE, LANES), bf16),
            pltpu.VMEM((steps, PIECE, LANES), bf16),
            pltpu.VMEM((pieces, PIECE, LANES), bf16),
            pltpu.VMEM((strips, reps, rows, LANES), bf16),
            pltpu.VMEM((strips, reps, rows, LANES), bf16),
            pltpu.VMEM((strips, rows, LANES), f32),
            pltpu.VMEM((rows, LANES), f32),
            pltpu.VMEM((rows, LANES), f32),
            dma((2,)),
            dma((2, reps)),
            dma((2, reps)),
            dma((2, reps)),
            dma((2, reps)),
            dma((steps,)),
            dma((steps,)),
            dma((steps,)),
            dma((steps,)),
            dma((strips, reps)),
            dma((strips, reps)),
            dma((2,)),
        ],
        compiler_params=pltpu.CompilerParams(
            collective_id=0, has_side_effects=True, vmem_limit_bytes=48 * 1024 * 1024
        ),
        cost_estimate=pl.CostEstimate(flops=flops, bytes_accessed=4 * rows * width, transcendentals=0),
    )(student, teacher)


def solution(mesh):
    placed = P(("loop", "rep"), "sec")
    return jax.shard_map(
        functools.partial(body, mesh.shape["loop"], mesh.shape["rep"]),
        mesh=mesh, in_specs=(placed, placed), out_specs=placed, check_vma=False,
    )
```

```python
import functools
import math

import jax
import jax.numpy as jnp
from jax import lax
from jax.experimental import pallas as pl
from jax.experimental.pallas import tpu as pltpu
from jax.sharding import PartitionSpec as P

MESH = pl.DeviceIdType.MESH
LANES = 128
PIECE = 256
LAG = 3
EARLY = 2
IDLE = 4
EPS = 1e-6


def kernel(
    loops, reps, coef, dup, s_hbm, t_hbm, out_ref,
    s_ref, t_ref, stat_tx, stat_rx, inv_keep, cols_all, cols_t, feats, feats_tx, own, right_tx, left_tx,
    from_left, from_right, full, part_tx, part_rx, part_own, inner_tx, inner_rx,
    load_sem, stat_sem, strip_send, strip_recv, gather_send, gather_recv, swap_send, swap_recv,
    right_send, right_recv, left_send, left_recv, part_send, part_recv, inner_sem,
):
    z = lax.axis_index("loop")
    b = lax.axis_index("rep")
    c = lax.axis_index("sec")
    rows, width = s_ref.shape
    pieces, total_rows, _ = feats.shape
    t_own = (pieces - 1) // 2
    strips = width // LANES
    steps = strips * pieces
    sibling = (z, b, 1 - c)
    has_left = z > 0
    has_right = z < loops - 1

    def peer(d):
        return lax.rem(b + d, reps)

    def span(q):
        return pl.ds(pl.multiple_of(q * rows, rows), rows)

    def lanes(j):
        return pl.ds(pl.multiple_of(j * LANES, LANES), LANES)

    load_s = pltpu.make_async_copy(s_hbm, s_ref, load_sem.at[0])
    load_t = pltpu.make_async_copy(t_hbm, t_ref, load_sem.at[1])
    load_s.start()
    load_t.start()
    barrier = pltpu.get_barrier_semaphore()
    for d in range(1, reps):
        pl.semaphore_signal(barrier, inc=1, device_id=(z, peer(d), c), device_id_type=MESH)
    pl.semaphore_signal(barrier, inc=1, device_id=sibling, device_id_type=MESH)

    @pl.when(has_left)
    def _():
        pl.semaphore_signal(barrier, inc=1, device_id=(z - 1, b, c), device_id_type=MESH)

    @pl.when(has_right)
    def _():
        pl.semaphore_signal(barrier, inc=1, device_id=(z + 1, b, c), device_id_type=MESH)

    load_s.wait()
    s32 = s_ref[...].astype(jnp.float32)
    part_s = jnp.sum(s32 * s32, axis=1, keepdims=True)
    load_t.wait()
    t32 = t_ref[...].astype(jnp.float32)
    part_t = jnp.sum(t32 * t32, axis=1, keepdims=True)
    lane = lax.broadcasted_iota(jnp.int32, (rows, LANES), 1)
    stat_tx[...] = jnp.where(lane < LANES // 2, part_s, part_t)

    pl.semaphore_wait(barrier, reps + has_left.astype(jnp.int32) + has_right.astype(jnp.int32))

    def remote(src, dst, send, recv, device):
        return pltpu.make_async_remote_copy(
            src_ref=src, dst_ref=dst, send_sem=send, recv_sem=recv,
            device_id=device, device_id_type=MESH,
        )

    stat = remote(stat_tx, stat_rx, stat_sem.at[0], stat_sem.at[1], sibling)
    stat.start()
    stat.wait()
    inv = lax.rsqrt(stat_tx[...] + stat_rx[...] + EPS)
    inv_s = inv[:, :1]
    inv_t = inv[:, LANES - 1:]
    inv_keep[...] = jnp.broadcast_to(inv_s, (rows, LANES))
    mine = span(b)
    cols_all[mine, :] = (s_ref[...].astype(jnp.float32) * inv_s).astype(jnp.bfloat16)

    def strip_to(d, j):
        at = lanes(j)
        return remote(cols_all.at[mine, at], cols_all.at[mine, at],
                      strip_send.at[j, d], strip_recv.at[j, d], (z, peer(d), c))

    def piece_to(d, p):
        return remote(feats_tx.at[peer(d), p], feats.at[2 * p, mine],
                      gather_send.at[p, d], gather_recv.at[p, d], (z, peer(d), c))

    for d in range(1, reps):
        strip_to(d, 0).start()
    for p in range(t_own):
        for q in range(reps):
            lo = (q * t_own + p) * PIECE
            feats_tx[q, p] = (t_ref[:, lo:lo + PIECE].astype(jnp.float32) * inv_t).astype(jnp.bfloat16)
        for d in range(1, reps):
            piece_to(d, p).start()
        feats[2 * p, mine, :] = feats_tx[b, p]
    for m in range(strips):
        for d in range(1, reps):
            j = lax.rem(peer(d) // dup + m, strips)

            @pl.when(j > 0)
            def _():
                strip_to(d, j).start()

    block = b // dup

    def came(d):
        return span(lax.rem(b - d + reps, reps))

    def piece_over(d, p):
        at = came(d)
        return remote(feats.at[2 * p, at], feats.at[2 * p + 1, at],
                      swap_send.at[p, d], swap_recv.at[p, d], sibling)

    def block_over(d):
        at = came(d)
        return remote(cols_all.at[at, lanes(block)], feats.at[pieces - 1, at, pl.ds(LANES, LANES)],
                      swap_send.at[t_own, d], swap_recv.at[t_own, d], sibling)

    def strip_in(j):
        for d in range(1, reps):
            strip_to(d, j).wait_recv()

    def turn(j):
        cols_t[j] = cols_all[:, j * LANES:(j + 1) * LANES].T

    def rightward(k):
        return remote(right_tx.at[k], from_left.at[k], right_send.at[k], right_recv.at[k], (z + 1, b, c))

    def leftward(k):
        return remote(left_tx.at[k], from_right.at[k], left_send.at[k], left_recv.at[k], (z - 1, b, c))

    def result(j, d):
        return remote(part_tx.at[j, peer(d)], part_rx.at[j, d],
                      part_send.at[j, d], part_recv.at[j, d], (z, peer(d), c))

    def produce(k):
        own[k] = jnp.dot(
            cols_t[k // pieces], feats[lax.rem(k, pieces)], preferred_element_type=jnp.float32
        )

    def up(k):
        @pl.when(has_left)
        def _():
            rightward(k).wait_recv()

        @pl.when(has_right)
        def _():
            @pl.when(has_left)
            def _():
                right_tx[k] = (own[k] + from_left[k].astype(jnp.float32)).astype(jnp.bfloat16)

            @pl.when(jnp.logical_not(has_left))
            def _():
                right_tx[k] = own[k].astype(jnp.bfloat16)
            rightward(k).start()

    def down(k):
        @pl.when(has_right)
        def _():
            leftward(k).wait_recv()

        @pl.when(has_left)
        def _():
            @pl.when(has_right)
            def _():
                left_tx[k] = (own[k] + from_right[k].astype(jnp.float32)).astype(jnp.bfloat16)

            @pl.when(jnp.logical_not(has_right))
            def _():
                left_tx[k] = own[k].astype(jnp.bfloat16)
            leftward(k).start()

    def across(left, right):
        return lax.dot_general(left, right, (((1,), (1,)), ((), ())), preferred_element_type=jnp.float32)

    def finish(k):
        j = k // pieces
        p = lax.rem(k, pieces)

        @pl.when(has_left)
        def _():
            own[k] = own[k] + from_left[k].astype(jnp.float32)

        @pl.when(has_right)
        def _():
            own[k] = own[k] + from_right[k].astype(jnp.float32)
        full[p] = own[k].astype(jnp.bfloat16)

        @pl.when(p == pieces - 1)
        def _():
            value = across(feats[pieces - 1], full[pieces - 1])
            if dup > 1:
                value = value * (1.0 / dup)
            for q in range(pieces - 1):
                value = value - across(feats[q], full[q])
            for q in range(reps):
                part_tx[j, q] = value[q * rows:(q + 1) * rows].astype(jnp.bfloat16)

                @pl.when(b == q)
                def _():
                    part_own[j] = value[q * rows:(q + 1) * rows]
            for d in range(1, reps):
                result(j, d).start()

    lag_up = LAG * z
    lag_down = LAG * (loops - 1 - z)
    lag_end = jnp.maximum(lag_up, lag_down)

    def chunk_at(i):
        k = jnp.where(i < EARLY, i, i - IDLE)
        idle = jnp.logical_and(i >= EARLY, i < EARLY + IDLE)
        return k, jnp.logical_and(jnp.logical_not(idle), jnp.logical_and(i >= 0, k < steps))

    def tick(i, carry):
        for lag, act in ((lag_up, up), (lag_down, down), (lag_end, finish)):
            k, live = chunk_at(i - lag)

            @pl.when(live)
            def _():
                act(k)
        return carry

    def made(k):
        produce(k)
        tick(k if k < EARLY else k + IDLE, 0)

    for p in range(t_own):
        piece_over(0, p).start()
    block_over(0).start()
    strip_in(0)
    turn(0)
    for p in range(t_own):
        for d in range(1, reps):
            piece_to(d, p).wait_recv()
            piece_over(d, p).start()
        made(2 * p)
        for d in range(reps):
            piece_over(d, p).wait_recv()
        made(2 * p + 1)
        if p == 0:
            lax.fori_loop(EARLY, EARLY + IDLE, tick, 0)

    @pl.when(block > 0)
    def _():
        strip_in(block)
    for d in range(1, reps):
        block_over(d).start()
    feats[pieces - 1, :, :LANES] = cols_all[:, lanes(block)]
    for d in range(reps):
        block_over(d).wait_recv()
    made(pieces - 1)
    for j in range(1, strips):
        @pl.when(block != j)
        def _():
            strip_in(j)
        turn(j)

        def make(k, carry):
            produce(k)
            return tick(k + IDLE, carry)

        lax.fori_loop(j * pieces, (j + 1) * pieces, make, 0)
    lax.fori_loop(steps + IDLE, steps + IDLE + LAG * (loops - 1), tick, 0)

    norm = cols_all[mine, :].astype(jnp.float32)
    inner = jnp.zeros((rows, 1), jnp.float32)
    grads = []
    for j in range(strips):
        grad = part_own[j]
        for d in range(1, reps):
            result(j, d).wait_recv()
            grad = grad + part_rx[j, d].astype(jnp.float32)
        grad = grad * coef
        grads.append(grad)
        inner = inner + jnp.sum(grad * norm[:, j * LANES:(j + 1) * LANES], axis=1, keepdims=True)
    inner_tx[...] = jnp.broadcast_to(inner, (rows, LANES))
    swap = remote(inner_tx, inner_rx, inner_sem.at[0], inner_sem.at[1], sibling)
    swap.start()
    swap.wait_recv()
    inner_all = inner_tx[...] + inner_rx[...]
    for j in range(strips):
        at = slice(j * LANES, (j + 1) * LANES)
        out_ref[:, at] = (grads[j] - inner_all * norm[:, at]) * inv_keep[...]

    swap.wait_send()
    for d in range(reps):
        for p in range(t_own):
            piece_over(d, p).wait_send()
            if d:
                piece_to(d, p).wait_send()
        block_over(d).wait_send()
    for j in range(strips):
        for d in range(1, reps):
            strip_to(d, j).wait_send()
            result(j, d).wait_send()

    def drain(k, carry):
        @pl.when(has_right)
        def _():
            rightward(k).wait_send()

        @pl.when(has_left)
        def _():
            leftward(k).wait_send()
        return carry

    lax.fori_loop(0, steps, drain, 0)


def body(loops, reps, student, teacher):
    rows, width = student.shape
    passages = rows * reps * loops
    coef = 32.0 * (2 * width) / math.sqrt(passages)
    dup = max(1, reps * LANES // width)
    t_own = teacher.shape[1] // (reps * PIECE)
    pieces = 1 + 2 * t_own
    strips = width // LANES
    steps = strips * pieces
    total = rows * reps
    f32, bf16 = jnp.float32, jnp.bfloat16
    dma = pltpu.SemaphoreType.DMA
    flops = 4 * total * pieces * PIECE * width
    return pl.pallas_call(
        functools.partial(kernel, loops, reps, coef, dup),
        out_shape=jax.ShapeDtypeStruct((rows, width), f32),
        in_specs=[pl.BlockSpec(memory_space=pltpu.HBM)] * 2,
        out_specs=pl.BlockSpec(memory_space=pltpu.VMEM),
        scratch_shapes=[
            pltpu.VMEM((rows, width), bf16),
            pltpu.VMEM((rows, teacher.shape[1]), bf16),
            pltpu.VMEM((rows, LANES), f32),
            pltpu.VMEM((rows, LANES), f32),
            pltpu.VMEM((rows, LANES), f32),
            pltpu.VMEM((total, width), bf16),
            pltpu.VMEM((strips, LANES, total), bf16),
            pltpu.VMEM((pieces, total, PIECE), bf16),
            pltpu.VMEM((reps, t_own, rows, PIECE), bf16),
            pltpu.VMEM((steps, LANES, PIECE), f32),
            pltpu.VMEM((steps, LANES, PIECE), bf16),
            pltpu.VMEM((steps, LANES, PIECE), bf16),
            pltpu.VMEM((steps, LANES, PIECE), bf16),
            pltpu.VMEM((steps, LANES, PIECE), bf16),
            pltpu.VMEM((pieces, LANES, PIECE), bf16),
            pltpu.VMEM((strips, reps, rows, LANES), bf16),
            pltpu.VMEM((strips, reps, rows, LANES), bf16),
            pltpu.VMEM((strips, rows, LANES), f32),
            pltpu.VMEM((rows, LANES), f32),
            pltpu.VMEM((rows, LANES), f32),
            dma((2,)),
            dma((2,)),
            dma((strips, reps)),
            dma((strips, reps)),
            dma((t_own, reps)),
            dma((t_own, reps)),
            dma((t_own + 1, reps)),
            dma((t_own + 1, reps)),
            dma((steps,)),
            dma((steps,)),
            dma((steps,)),
            dma((steps,)),
            dma((strips, reps)),
            dma((strips, reps)),
            dma((2,)),
        ],
        compiler_params=pltpu.CompilerParams(
            collective_id=0, has_side_effects=True, vmem_limit_bytes=48 * 1024 * 1024
        ),
        cost_estimate=pl.CostEstimate(flops=flops, bytes_accessed=4 * rows * width, transcendentals=0),
    )(student, teacher)


def solution(mesh):
    placed = P(("loop", "rep"), "sec")
    return jax.shard_map(
        functools.partial(body, mesh.shape["loop"], mesh.shape["rep"]),
        mesh=mesh, in_specs=(placed, placed), out_specs=placed, check_vma=False,
    )
```

```python
import functools
import math

import jax
import jax.numpy as jnp
from jax import lax
from jax.experimental import pallas as pl
from jax.experimental.pallas import tpu as pltpu
from jax.sharding import PartitionSpec as P

MESH = pl.DeviceIdType.MESH
LANES = 128
PIECE = 256
LAG = 3
EARLY = 2
IDLE = 4
EPS = 1e-6


def kernel(
    loops, reps, coef, dup, s_hbm, t_hbm, out_ref,
    s_ref, t_ref, stat_tx, stat_rx, inv_keep, cols_all, cols_t, feats, feats_tx, own, right_tx, left_tx,
    from_left, from_right, full, part_tx, part_rx, part_own, inner_tx, inner_rx,
    load_sem, stat_sem, strip_send, strip_recv, gather_send, gather_recv, swap_send, swap_recv,
    right_send, right_recv, left_send, left_recv, part_send, part_recv, inner_sem,
):
    z = lax.axis_index("loop")
    b = lax.axis_index("rep")
    c = lax.axis_index("sec")
    rows, width = s_ref.shape
    pieces, total_rows, _ = feats.shape
    t_own = (pieces - 1) // 2
    strips = width // LANES
    steps = strips * pieces
    sibling = (z, b, 1 - c)
    has_left = z > 0
    has_right = z < loops - 1

    def peer(d):
        return lax.rem(b + d, reps)

    def span(q):
        return pl.ds(pl.multiple_of(q * rows, rows), rows)

    def lanes(j):
        return pl.ds(pl.multiple_of(j * LANES, LANES), LANES)

    load_s = pltpu.make_async_copy(s_hbm, s_ref, load_sem.at[0])
    load_t = pltpu.make_async_copy(t_hbm, t_ref, load_sem.at[1])
    load_s.start()
    load_t.start()
    barrier = pltpu.get_barrier_semaphore()
    for d in range(1, reps):
        pl.semaphore_signal(barrier, inc=1, device_id=(z, peer(d), c), device_id_type=MESH)
    pl.semaphore_signal(barrier, inc=1, device_id=sibling, device_id_type=MESH)

    @pl.when(has_left)
    def _():
        pl.semaphore_signal(barrier, inc=1, device_id=(z - 1, b, c), device_id_type=MESH)

    @pl.when(has_right)
    def _():
        pl.semaphore_signal(barrier, inc=1, device_id=(z + 1, b, c), device_id_type=MESH)

    load_s.wait()
    s32 = s_ref[...].astype(jnp.float32)
    part_s = jnp.sum(s32 * s32, axis=1, keepdims=True)
    load_t.wait()
    t32 = t_ref[...].astype(jnp.float32)
    part_t = jnp.sum(t32 * t32, axis=1, keepdims=True)
    lane = lax.broadcasted_iota(jnp.int32, (rows, LANES), 1)
    stat_tx[...] = jnp.where(lane < LANES // 2, part_s, part_t)

    pl.semaphore_wait(barrier, reps + has_left.astype(jnp.int32) + has_right.astype(jnp.int32))

    def remote(src, dst, send, recv, device):
        return pltpu.make_async_remote_copy(
            src_ref=src, dst_ref=dst, send_sem=send, recv_sem=recv,
            device_id=device, device_id_type=MESH,
        )

    stat = remote(stat_tx, stat_rx, stat_sem.at[0], stat_sem.at[1], sibling)
    stat.start()
    stat.wait()
    inv = lax.rsqrt(stat_tx[...] + stat_rx[...] + EPS)
    inv_s = inv[:, :1]
    inv_t = inv[:, LANES - 1:]
    inv_keep[...] = jnp.broadcast_to(inv_s, (rows, LANES))
    mine = span(b)
    cols_all[mine, :] = (s_ref[...].astype(jnp.float32) * inv_s).astype(jnp.bfloat16)

    def strip_to(d, j):
        at = lanes(j)
        return remote(cols_all.at[mine, at], cols_all.at[mine, at],
                      strip_send.at[j, d], strip_recv.at[j, d], (z, peer(d), c))

    def piece_to(d, p):
        return remote(feats_tx.at[peer(d), p], feats.at[2 * p, mine],
                      gather_send.at[p, d], gather_recv.at[p, d], (z, peer(d), c))

    for d in range(1, reps):
        strip_to(d, 0).start()
    for p in range(t_own):
        for q in range(reps):
            lo = (q * t_own + p) * PIECE
            feats_tx[q, p] = (t_ref[:, lo:lo + PIECE].astype(jnp.float32) * inv_t).astype(jnp.bfloat16)
        if p == 0:
            for d in range(1, reps):
                piece_to(d, 0).start()
        feats[2 * p, mine, :] = feats_tx[b, p]

    def send_strips(m):
        for d in range(1, reps):
            j = lax.rem(peer(d) // dup + m, strips)

            @pl.when(j > 0)
            def _():
                strip_to(d, j).start()

    block = b // dup

    def came(d):
        return span(lax.rem(b - d + reps, reps))

    def piece_over(d, p):
        at = came(d)
        return remote(feats.at[2 * p, at], feats.at[2 * p + 1, at],
                      swap_send.at[p, d], swap_recv.at[p, d], sibling)

    def block_over(d):
        at = came(d)
        return remote(cols_all.at[at, lanes(block)], feats.at[pieces - 1, at, pl.ds(LANES, LANES)],
                      swap_send.at[t_own, d], swap_recv.at[t_own, d], sibling)

    def strip_in(j):
        for d in range(1, reps):
            strip_to(d, j).wait_recv()

    def turn(j):
        cols_t[j] = cols_all[:, j * LANES:(j + 1) * LANES].T

    def rightward(k):
        return remote(right_tx.at[k], from_left.at[k], right_send.at[k], right_recv.at[k], (z + 1, b, c))

    def leftward(k):
        return remote(left_tx.at[k], from_right.at[k], left_send.at[k], left_recv.at[k], (z - 1, b, c))

    def result(j, d):
        return remote(part_tx.at[j, peer(d)], part_rx.at[j, d],
                      part_send.at[j, d], part_recv.at[j, d], (z, peer(d), c))

    def produce(k):
        own[k] = jnp.dot(
            cols_t[k // pieces], feats[lax.rem(k, pieces)], preferred_element_type=jnp.float32
        )

    def up(k):
        @pl.when(has_left)
        def _():
            rightward(k).wait_recv()

        @pl.when(has_right)
        def _():
            @pl.when(has_left)
            def _():
                right_tx[k] = (own[k] + from_left[k].astype(jnp.float32)).astype(jnp.bfloat16)

            @pl.when(jnp.logical_not(has_left))
            def _():
                right_tx[k] = own[k].astype(jnp.bfloat16)
            rightward(k).start()

    def down(k):
        @pl.when(has_right)
        def _():
            leftward(k).wait_recv()

        @pl.when(has_left)
        def _():
            @pl.when(has_right)
            def _():
                left_tx[k] = (own[k] + from_right[k].astype(jnp.float32)).astype(jnp.bfloat16)

            @pl.when(jnp.logical_not(has_right))
            def _():
                left_tx[k] = own[k].astype(jnp.bfloat16)
            leftward(k).start()

    def across(left, right):
        return lax.dot_general(left, right, (((1,), (1,)), ((), ())), preferred_element_type=jnp.float32)

    def finish(k):
        j = k // pieces
        p = lax.rem(k, pieces)

        @pl.when(has_left)
        def _():
            own[k] = own[k] + from_left[k].astype(jnp.float32)

        @pl.when(has_right)
        def _():
            own[k] = own[k] + from_right[k].astype(jnp.float32)
        full[p] = own[k].astype(jnp.bfloat16)

        @pl.when(p == pieces - 1)
        def _():
            value = across(feats[pieces - 1], full[pieces - 1])
            if dup > 1:
                value = value * (1.0 / dup)
            for q in range(pieces - 1):
                value = value - across(feats[q], full[q])
            for q in range(reps):
                part_tx[j, q] = value[q * rows:(q + 1) * rows].astype(jnp.bfloat16)

                @pl.when(b == q)
                def _():
                    part_own[j] = value[q * rows:(q + 1) * rows]
            for d in range(1, reps):
                result(j, d).start()

    lag_up = LAG * z
    lag_down = LAG * (loops - 1 - z)
    lag_end = jnp.maximum(lag_up, lag_down)

    def chunk_at(i):
        k = jnp.where(i < EARLY, i, i - IDLE)
        idle = jnp.logical_and(i >= EARLY, i < EARLY + IDLE)
        return k, jnp.logical_and(jnp.logical_not(idle), jnp.logical_and(i >= 0, k < steps))

    def tick(i, carry):
        for lag, act in ((lag_up, up), (lag_down, down), (lag_end, finish)):
            k, live = chunk_at(i - lag)

            @pl.when(live)
            def _():
                act(k)
        return carry

    def made(k):
        produce(k)
        tick(k if k < EARLY else k + IDLE, 0)

    for p in range(t_own):
        piece_over(0, p).start()
    block_over(0).start()
    strip_in(0)
    for p in range(1, t_own):
        for d in range(1, reps):
            piece_to(d, p).start()
    turn(0)
    for p in range(t_own):
        for d in range(1, reps):
            piece_to(d, p).wait_recv()
            piece_over(d, p).start()
        if p == 0:
            send_strips(0)
        if p == t_own - 1:
            for m in range(1, strips):
                send_strips(m)
        made(2 * p)
        for d in range(reps):
            piece_over(d, p).wait_recv()
        made(2 * p + 1)
        if p == 0:
            lax.fori_loop(EARLY, EARLY + IDLE, tick, 0)

    @pl.when(block > 0)
    def _():
        strip_in(block)
    for d in range(1, reps):
        block_over(d).start()
    feats[pieces - 1, :, :LANES] = cols_all[:, lanes(block)]
    for d in range(reps):
        block_over(d).wait_recv()
    made(pieces - 1)
    for j in range(1, strips):
        @pl.when(block != j)
        def _():
            strip_in(j)
        turn(j)

        def make(k, carry):
            produce(k)
            return tick(k + IDLE, carry)

        lax.fori_loop(j * pieces, (j + 1) * pieces, make, 0)
    lax.fori_loop(steps + IDLE, steps + IDLE + LAG * (loops - 1), tick, 0)

    norm = cols_all[mine, :].astype(jnp.float32)
    inner = jnp.zeros((rows, 1), jnp.float32)
    grads = []
    for j in range(strips):
        grad = part_own[j]
        for d in range(1, reps):
            result(j, d).wait_recv()
            grad = grad + part_rx[j, d].astype(jnp.float32)
        grad = grad * coef
        grads.append(grad)
        inner = inner + jnp.sum(grad * norm[:, j * LANES:(j + 1) * LANES], axis=1, keepdims=True)
    inner_tx[...] = jnp.broadcast_to(inner, (rows, LANES))
    swap = remote(inner_tx, inner_rx, inner_sem.at[0], inner_sem.at[1], sibling)
    swap.start()
    swap.wait_recv()
    inner_all = inner_tx[...] + inner_rx[...]
    for j in range(strips):
        at = slice(j * LANES, (j + 1) * LANES)
        out_ref[:, at] = (grads[j] - inner_all * norm[:, at]) * inv_keep[...]

    swap.wait_send()
    for d in range(reps):
        for p in range(t_own):
            piece_over(d, p).wait_send()
            if d:
                piece_to(d, p).wait_send()
        block_over(d).wait_send()
    for j in range(strips):
        for d in range(1, reps):
            strip_to(d, j).wait_send()
            result(j, d).wait_send()

    def drain(k, carry):
        @pl.when(has_right)
        def _():
            rightward(k).wait_send()

        @pl.when(has_left)
        def _():
            leftward(k).wait_send()
        return carry

    lax.fori_loop(0, steps, drain, 0)


def body(loops, reps, student, teacher):
    rows, width = student.shape
    passages = rows * reps * loops
    coef = 32.0 * (2 * width) / math.sqrt(passages)
    dup = max(1, reps * LANES // width)
    t_own = teacher.shape[1] // (reps * PIECE)
    pieces = 1 + 2 * t_own
    strips = width // LANES
    steps = strips * pieces
    total = rows * reps
    f32, bf16 = jnp.float32, jnp.bfloat16
    dma = pltpu.SemaphoreType.DMA
    flops = 4 * total * pieces * PIECE * width
    return pl.pallas_call(
        functools.partial(kernel, loops, reps, coef, dup),
        out_shape=jax.ShapeDtypeStruct((rows, width), f32),
        in_specs=[pl.BlockSpec(memory_space=pltpu.HBM)] * 2,
        out_specs=pl.BlockSpec(memory_space=pltpu.VMEM),
        scratch_shapes=[
            pltpu.VMEM((rows, width), bf16),
            pltpu.VMEM((rows, teacher.shape[1]), bf16),
            pltpu.VMEM((rows, LANES), f32),
            pltpu.VMEM((rows, LANES), f32),
            pltpu.VMEM((rows, LANES), f32),
            pltpu.VMEM((total, width), bf16),
            pltpu.VMEM((strips, LANES, total), bf16),
            pltpu.VMEM((pieces, total, PIECE), bf16),
            pltpu.VMEM((reps, t_own, rows, PIECE), bf16),
            pltpu.VMEM((steps, LANES, PIECE), f32),
            pltpu.VMEM((steps, LANES, PIECE), bf16),
            pltpu.VMEM((steps, LANES, PIECE), bf16),
            pltpu.VMEM((steps, LANES, PIECE), bf16),
            pltpu.VMEM((steps, LANES, PIECE), bf16),
            pltpu.VMEM((pieces, LANES, PIECE), bf16),
            pltpu.VMEM((strips, reps, rows, LANES), bf16),
            pltpu.VMEM((strips, reps, rows, LANES), bf16),
            pltpu.VMEM((strips, rows, LANES), f32),
            pltpu.VMEM((rows, LANES), f32),
            pltpu.VMEM((rows, LANES), f32),
            dma((2,)),
            dma((2,)),
            dma((strips, reps)),
            dma((strips, reps)),
            dma((t_own, reps)),
            dma((t_own, reps)),
            dma((t_own + 1, reps)),
            dma((t_own + 1, reps)),
            dma((steps,)),
            dma((steps,)),
            dma((steps,)),
            dma((steps,)),
            dma((strips, reps)),
            dma((strips, reps)),
            dma((2,)),
        ],
        compiler_params=pltpu.CompilerParams(
            collective_id=0, has_side_effects=True, vmem_limit_bytes=64 * 1024 * 1024
        ),
        cost_estimate=pl.CostEstimate(flops=flops, bytes_accessed=4 * rows * width, transcendentals=0),
    )(student, teacher)


def solution(mesh):
    placed = P(("loop", "rep"), "sec")
    return jax.shard_map(
        functools.partial(body, mesh.shape["loop"], mesh.shape["rep"]),
        mesh=mesh, in_specs=(placed, placed), out_specs=placed, check_vma=False,
    )
```

```python
import functools
import math

import jax
import jax.numpy as jnp
from jax import lax
from jax.experimental import pallas as pl
from jax.experimental.pallas import tpu as pltpu
from jax.sharding import PartitionSpec as P

MESH = pl.DeviceIdType.MESH
LANES = 128
PIECE = 256
LAG = 6
EARLY = 2
IDLE = 4
EPS = 1e-6


def kernel(
    loops, reps, coef, dup, s_hbm, t_hbm, out_ref,
    s_ref, t_ref, stat_tx, stat_rx, inv_keep, cols_all, cols_t, feats, feats_tx, own, right_tx, left_tx,
    from_left, from_right, full, part_tx, part_rx, part_own, inner_tx, inner_rx,
    load_sem, stat_sem, strip_send, strip_recv, gather_send, gather_recv, swap_send, swap_recv,
    right_send, right_recv, left_send, left_recv, part_send, part_recv, inner_sem,
):
    z = lax.axis_index("loop")
    b = lax.axis_index("rep")
    c = lax.axis_index("sec")
    rows, width = s_ref.shape
    pieces, total_rows, _ = feats.shape
    t_own = (pieces - 1) // 2
    strips = width // LANES
    steps = strips * pieces
    sibling = (z, b, 1 - c)
    has_left = z > 0
    has_right = z < loops - 1

    def peer(d):
        return lax.rem(b + d, reps)

    def span(q):
        return pl.ds(pl.multiple_of(q * rows, rows), rows)

    def lanes(j):
        return pl.ds(pl.multiple_of(j * LANES, LANES), LANES)

    load_s = pltpu.make_async_copy(s_hbm, s_ref, load_sem.at[0])
    load_t = pltpu.make_async_copy(t_hbm, t_ref, load_sem.at[1])
    load_s.start()
    load_t.start()
    barrier = pltpu.get_barrier_semaphore()
    for d in range(1, reps):
        pl.semaphore_signal(barrier, inc=1, device_id=(z, peer(d), c), device_id_type=MESH)
    pl.semaphore_signal(barrier, inc=1, device_id=sibling, device_id_type=MESH)

    @pl.when(has_left)
    def _():
        pl.semaphore_signal(barrier, inc=1, device_id=(z - 1, b, c), device_id_type=MESH)

    @pl.when(has_right)
    def _():
        pl.semaphore_signal(barrier, inc=1, device_id=(z + 1, b, c), device_id_type=MESH)

    load_s.wait()
    s32 = s_ref[...].astype(jnp.float32)
    part_s = jnp.sum(s32 * s32, axis=1, keepdims=True)
    load_t.wait()
    t32 = t_ref[...].astype(jnp.float32)
    part_t = jnp.sum(t32 * t32, axis=1, keepdims=True)
    lane = lax.broadcasted_iota(jnp.int32, (rows, LANES), 1)
    stat_tx[...] = jnp.where(lane < LANES // 2, part_s, part_t)

    pl.semaphore_wait(barrier, reps + has_left.astype(jnp.int32) + has_right.astype(jnp.int32))

    def remote(src, dst, send, recv, device):
        return pltpu.make_async_remote_copy(
            src_ref=src, dst_ref=dst, send_sem=send, recv_sem=recv,
            device_id=device, device_id_type=MESH,
        )

    stat = remote(stat_tx, stat_rx, stat_sem.at[0], stat_sem.at[1], sibling)
    stat.start()
    stat.wait()
    inv = lax.rsqrt(stat_tx[...] + stat_rx[...] + EPS)
    inv_s = inv[:, :1]
    inv_t = inv[:, LANES - 1:]
    inv_keep[...] = jnp.broadcast_to(inv_s, (rows, LANES))
    mine = span(b)
    cols_all[mine, :] = (s_ref[...].astype(jnp.float32) * inv_s).astype(jnp.bfloat16)

    def strip_to(d, j):
        at = lanes(j)
        return remote(cols_all.at[mine, at], cols_all.at[mine, at],
                      strip_send.at[j, d], strip_recv.at[j, d], (z, peer(d), c))

    def piece_to(d, p):
        return remote(feats_tx.at[peer(d), p], feats.at[2 * p, mine],
                      gather_send.at[p, d], gather_recv.at[p, d], (z, peer(d), c))

    for d in range(1, reps):
        strip_to(d, 0).start()
    for p in range(t_own):
        for q in range(reps):
            lo = (q * t_own + p) * PIECE
            feats_tx[q, p] = (t_ref[:, lo:lo + PIECE].astype(jnp.float32) * inv_t).astype(jnp.bfloat16)
        if p == 0:
            for d in range(1, reps):
                piece_to(d, 0).start()
        feats[2 * p, mine, :] = feats_tx[b, p]

    def send_strips(m):
        for d in range(1, reps):
            j = lax.rem(peer(d) // dup + m, strips)

            @pl.when(j > 0)
            def _():
                strip_to(d, j).start()

    block = b // dup

    def came(d):
        return span(lax.rem(b - d + reps, reps))

    def piece_over(d, p):
        at = came(d)
        return remote(feats.at[2 * p, at], feats.at[2 * p + 1, at],
                      swap_send.at[p, d], swap_recv.at[p, d], sibling)

    def block_over(d):
        at = came(d)
        return remote(cols_all.at[at, lanes(block)], feats.at[pieces - 1, at, pl.ds(LANES, LANES)],
                      swap_send.at[t_own, d], swap_recv.at[t_own, d], sibling)

    def strip_in(j):
        for d in range(1, reps):
            strip_to(d, j).wait_recv()

    def turn(j):
        cols_t[j] = cols_all[:, j * LANES:(j + 1) * LANES].T

    def rightward(k):
        return remote(right_tx.at[k], from_left.at[k], right_send.at[k], right_recv.at[k], (z + 1, b, c))

    def leftward(k):
        return remote(left_tx.at[k], from_right.at[k], left_send.at[k], left_recv.at[k], (z - 1, b, c))

    def result(j, d):
        return remote(part_tx.at[j, peer(d)], part_rx.at[j, d],
                      part_send.at[j, d], part_recv.at[j, d], (z, peer(d), c))

    def produce(k):
        own[k] = jnp.dot(
            cols_t[k // pieces], feats[lax.rem(k, pieces)], preferred_element_type=jnp.float32
        )

    def up(k):
        @pl.when(has_left)
        def _():
            rightward(k).wait_recv()

        @pl.when(has_right)
        def _():
            @pl.when(has_left)
            def _():
                right_tx[k] = (own[k] + from_left[k].astype(jnp.float32)).astype(jnp.bfloat16)

            @pl.when(jnp.logical_not(has_left))
            def _():
                right_tx[k] = own[k].astype(jnp.bfloat16)
            rightward(k).start()

    def down(k):
        @pl.when(has_right)
        def _():
            leftward(k).wait_recv()

        @pl.when(has_left)
        def _():
            @pl.when(has_right)
            def _():
                left_tx[k] = (own[k] + from_right[k].astype(jnp.float32)).astype(jnp.bfloat16)

            @pl.when(jnp.logical_not(has_right))
            def _():
                left_tx[k] = own[k].astype(jnp.bfloat16)
            leftward(k).start()

    def across(left, right):
        return lax.dot_general(left, right, (((1,), (1,)), ((), ())), preferred_element_type=jnp.float32)

    def finish(k):
        j = k // pieces
        p = lax.rem(k, pieces)

        @pl.when(has_left)
        def _():
            own[k] = own[k] + from_left[k].astype(jnp.float32)

        @pl.when(has_right)
        def _():
            own[k] = own[k] + from_right[k].astype(jnp.float32)
        full[p] = own[k].astype(jnp.bfloat16)

        @pl.when(p == pieces - 1)
        def _():
            value = across(feats[pieces - 1], full[pieces - 1])
            if dup > 1:
                value = value * (1.0 / dup)
            for q in range(pieces - 1):
                value = value - across(feats[q], full[q])
            for q in range(reps):
                part_tx[j, q] = value[q * rows:(q + 1) * rows].astype(jnp.bfloat16)

                @pl.when(b == q)
                def _():
                    part_own[j] = value[q * rows:(q + 1) * rows]
            for d in range(1, reps):
                result(j, d).start()

    lag_up = LAG * z
    lag_down = LAG * (loops - 1 - z)
    lag_end = jnp.maximum(lag_up, lag_down)

    def chunk_at(i):
        k = jnp.where(i < EARLY, i, i - IDLE)
        idle = jnp.logical_and(i >= EARLY, i < EARLY + IDLE)
        return k, jnp.logical_and(jnp.logical_not(idle), jnp.logical_and(i >= 0, k < steps))

    def tick(i, carry):
        for lag, act in ((lag_up, up), (lag_down, down), (lag_end, finish)):
            k, live = chunk_at(i - lag)

            @pl.when(live)
            def _():
                act(k)
        return carry

    def made(k):
        produce(k)
        tick(k if k < EARLY else k + IDLE, 0)

    for p in range(t_own):
        piece_over(0, p).start()
    block_over(0).start()
    strip_in(0)
    for p in range(1, t_own):
        for d in range(1, reps):
            piece_to(d, p).start()
    turn(0)
    for p in range(t_own):
        for d in range(1, reps):
            piece_to(d, p).wait_recv()
            piece_over(d, p).start()
        if p == 0:
            send_strips(0)
        if p == t_own - 1:
            for m in range(1, strips):
                send_strips(m)
        made(2 * p)
        for d in range(reps):
            piece_over(d, p).wait_recv()
        made(2 * p + 1)
        if p == 0:
            lax.fori_loop(EARLY, EARLY + IDLE, tick, 0)

    @pl.when(block > 0)
    def _():
        strip_in(block)
    for d in range(1, reps):
        block_over(d).start()
    feats[pieces - 1, :, :LANES] = cols_all[:, lanes(block)]
    for d in range(reps):
        block_over(d).wait_recv()
    made(pieces - 1)
    for j in range(1, strips):
        @pl.when(block != j)
        def _():
            strip_in(j)
        turn(j)

        def make(k, carry):
            produce(k)
            return tick(k + IDLE, carry)

        lax.fori_loop(j * pieces, (j + 1) * pieces, make, 0)
    lax.fori_loop(steps + IDLE, steps + IDLE + LAG * (loops - 1), tick, 0)

    norm = cols_all[mine, :].astype(jnp.float32)
    inner = jnp.zeros((rows, 1), jnp.float32)
    grads = []
    for j in range(strips):
        grad = part_own[j]
        for d in range(1, reps):
            result(j, d).wait_recv()
            grad = grad + part_rx[j, d].astype(jnp.float32)
        grad = grad * coef
        grads.append(grad)
        inner = inner + jnp.sum(grad * norm[:, j * LANES:(j + 1) * LANES], axis=1, keepdims=True)
    inner_tx[...] = jnp.broadcast_to(inner, (rows, LANES))
    swap = remote(inner_tx, inner_rx, inner_sem.at[0], inner_sem.at[1], sibling)
    swap.start()
    swap.wait_recv()
    inner_all = inner_tx[...] + inner_rx[...]
    for j in range(strips):
        at = slice(j * LANES, (j + 1) * LANES)
        out_ref[:, at] = (grads[j] - inner_all * norm[:, at]) * inv_keep[...]

    swap.wait_send()
    for d in range(reps):
        for p in range(t_own):
            piece_over(d, p).wait_send()
            if d:
                piece_to(d, p).wait_send()
        block_over(d).wait_send()
    for j in range(strips):
        for d in range(1, reps):
            strip_to(d, j).wait_send()
            result(j, d).wait_send()

    def drain(k, carry):
        @pl.when(has_right)
        def _():
            rightward(k).wait_send()

        @pl.when(has_left)
        def _():
            leftward(k).wait_send()
        return carry

    lax.fori_loop(0, steps, drain, 0)


def body(loops, reps, student, teacher):
    rows, width = student.shape
    passages = rows * reps * loops
    coef = 32.0 * (2 * width) / math.sqrt(passages)
    dup = max(1, reps * LANES // width)
    t_own = teacher.shape[1] // (reps * PIECE)
    pieces = 1 + 2 * t_own
    strips = width // LANES
    steps = strips * pieces
    total = rows * reps
    f32, bf16 = jnp.float32, jnp.bfloat16
    dma = pltpu.SemaphoreType.DMA
    flops = 4 * total * pieces * PIECE * width
    return pl.pallas_call(
        functools.partial(kernel, loops, reps, coef, dup),
        out_shape=jax.ShapeDtypeStruct((rows, width), f32),
        in_specs=[pl.BlockSpec(memory_space=pltpu.HBM)] * 2,
        out_specs=pl.BlockSpec(memory_space=pltpu.VMEM),
        scratch_shapes=[
            pltpu.VMEM((rows, width), bf16),
            pltpu.VMEM((rows, teacher.shape[1]), bf16),
            pltpu.VMEM((rows, LANES), f32),
            pltpu.VMEM((rows, LANES), f32),
            pltpu.VMEM((rows, LANES), f32),
            pltpu.VMEM((total, width), bf16),
            pltpu.VMEM((strips, LANES, total), bf16),
            pltpu.VMEM((pieces, total, PIECE), bf16),
            pltpu.VMEM((reps, t_own, rows, PIECE), bf16),
            pltpu.VMEM((steps, LANES, PIECE), f32),
            pltpu.VMEM((steps, LANES, PIECE), bf16),
            pltpu.VMEM((steps, LANES, PIECE), bf16),
            pltpu.VMEM((steps, LANES, PIECE), bf16),
            pltpu.VMEM((steps, LANES, PIECE), bf16),
            pltpu.VMEM((pieces, LANES, PIECE), bf16),
            pltpu.VMEM((strips, reps, rows, LANES), bf16),
            pltpu.VMEM((strips, reps, rows, LANES), bf16),
            pltpu.VMEM((strips, rows, LANES), f32),
            pltpu.VMEM((rows, LANES), f32),
            pltpu.VMEM((rows, LANES), f32),
            dma((2,)),
            dma((2,)),
            dma((strips, reps)),
            dma((strips, reps)),
            dma((t_own, reps)),
            dma((t_own, reps)),
            dma((t_own + 1, reps)),
            dma((t_own + 1, reps)),
            dma((steps,)),
            dma((steps,)),
            dma((steps,)),
            dma((steps,)),
            dma((strips, reps)),
            dma((strips, reps)),
            dma((2,)),
        ],
        compiler_params=pltpu.CompilerParams(
            collective_id=0, has_side_effects=True, vmem_limit_bytes=65024 * 1024 - 128 * 1024
        ),
        cost_estimate=pl.CostEstimate(flops=flops, bytes_accessed=4 * rows * width, transcendentals=0),
    )(student, teacher)


def solution(mesh):
    placed = P(("loop", "rep"), "sec")
    return jax.shard_map(
        functools.partial(body, mesh.shape["loop"], mesh.shape["rep"]),
        mesh=mesh, in_specs=(placed, placed), out_specs=placed, check_vma=False,
    )
```

```python
import functools
import math

import jax
import jax.numpy as jnp
from jax import lax
from jax.experimental import pallas as pl
from jax.experimental.pallas import tpu as pltpu
from jax.sharding import PartitionSpec as P

MESH = pl.DeviceIdType.MESH
LANES = 128
PIECE = 256
LAG = 3
IDLE = 6
EPS = 1e-6


def kernel(
    loops, reps, coef, dup, s_hbm, t_hbm, out_ref,
    s_ref, t_ref, stat_tx, stat_rx, inv_keep, cols_all, cols_t, feats, feats_tx, own, right_tx, left_tx,
    from_left, from_right, acc, part_tx, part_rx, part_own, inner_tx, inner_rx,
    load_sem, stat_sem, strip_send, strip_recv, gather_send, gather_recv, swap_send, swap_recv,
    right_send, right_recv, left_send, left_recv, part_send, part_recv, inner_sem,
):
    z = lax.axis_index("loop")
    b = lax.axis_index("rep")
    c = lax.axis_index("sec")
    rows, width = s_ref.shape
    pieces, total_rows, _ = feats.shape
    t_own = (pieces - 1) // 2
    strips = width // LANES
    steps = strips * pieces
    early = 2 * strips
    later = pieces - 2
    sibling = (z, b, 1 - c)
    has_left = z > 0
    has_right = z < loops - 1

    def peer(d):
        return lax.rem(b + d, reps)

    def span(q):
        return pl.ds(pl.multiple_of(q * rows, rows), rows)

    def lanes(j):
        return pl.ds(pl.multiple_of(j * LANES, LANES), LANES)

    load_s = pltpu.make_async_copy(s_hbm, s_ref, load_sem.at[0])
    load_t = pltpu.make_async_copy(t_hbm, t_ref, load_sem.at[1])
    load_s.start()
    load_t.start()
    barrier = pltpu.get_barrier_semaphore()
    for d in range(1, reps):
        pl.semaphore_signal(barrier, inc=1, device_id=(z, peer(d), c), device_id_type=MESH)
    pl.semaphore_signal(barrier, inc=1, device_id=sibling, device_id_type=MESH)

    @pl.when(has_left)
    def _():
        pl.semaphore_signal(barrier, inc=1, device_id=(z - 1, b, c), device_id_type=MESH)

    @pl.when(has_right)
    def _():
        pl.semaphore_signal(barrier, inc=1, device_id=(z + 1, b, c), device_id_type=MESH)

    load_s.wait()
    s32 = s_ref[...].astype(jnp.float32)
    part_s = jnp.sum(s32 * s32, axis=1, keepdims=True)
    load_t.wait()
    t32 = t_ref[...].astype(jnp.float32)
    part_t = jnp.sum(t32 * t32, axis=1, keepdims=True)
    lane = lax.broadcasted_iota(jnp.int32, (rows, LANES), 1)
    stat_tx[...] = jnp.where(lane < LANES // 2, part_s, part_t)

    pl.semaphore_wait(barrier, reps + has_left.astype(jnp.int32) + has_right.astype(jnp.int32))

    def remote(src, dst, send, recv, device):
        return pltpu.make_async_remote_copy(
            src_ref=src, dst_ref=dst, send_sem=send, recv_sem=recv,
            device_id=device, device_id_type=MESH,
        )

    stat = remote(stat_tx, stat_rx, stat_sem.at[0], stat_sem.at[1], sibling)
    stat.start()
    stat.wait()
    inv = lax.rsqrt(stat_tx[...] + stat_rx[...] + EPS)
    inv_s = inv[:, :1]
    inv_t = inv[:, LANES - 1:]
    inv_keep[...] = jnp.broadcast_to(inv_s, (rows, LANES))
    mine = span(b)
    cols_all[mine, :] = (s_ref[...].astype(jnp.float32) * inv_s).astype(jnp.bfloat16)

    def strip_to(d, j):
        at = lanes(j)
        return remote(cols_all.at[mine, at], cols_all.at[mine, at],
                      strip_send.at[j, d], strip_recv.at[j, d], (z, peer(d), c))

    def piece_to(d, p):
        return remote(feats_tx.at[peer(d), p], feats.at[2 * p, mine],
                      gather_send.at[p, d], gather_recv.at[p, d], (z, peer(d), c))

    def send_strip(j):
        if j < strips:
            for d in range(1, reps):
                strip_to(d, j).start()

    def send_piece(p):
        for d in range(1, reps):
            piece_to(d, p).start()

    send_strip(0)
    for p in range(t_own):
        for q in range(reps):
            lo = (q * t_own + p) * PIECE
            feats_tx[q, p] = (t_ref[:, lo:lo + PIECE].astype(jnp.float32) * inv_t).astype(jnp.bfloat16)
        if p == 0:
            send_piece(0)
            send_strip(1)
        feats[2 * p, mine, :] = feats_tx[b, p]

    block = b // dup

    def came(d):
        return span(lax.rem(b - d + reps, reps))

    def piece_over(d, p):
        at = came(d)
        return remote(feats.at[2 * p, at], feats.at[2 * p + 1, at],
                      swap_send.at[p, d], swap_recv.at[p, d], sibling)

    def block_over(d):
        at = came(d)
        return remote(cols_all.at[at, lanes(block)], feats.at[pieces - 1, at, pl.ds(LANES, LANES)],
                      swap_send.at[t_own, d], swap_recv.at[t_own, d], sibling)

    def strip_in(j):
        for d in range(1, reps):
            strip_to(d, j).wait_recv()

    def turn(j):
        cols_t[j] = cols_all[:, j * LANES:(j + 1) * LANES].T

    def rightward(k):
        return remote(right_tx.at[k], from_left.at[k], right_send.at[k], right_recv.at[k], (z + 1, b, c))

    def leftward(k):
        return remote(left_tx.at[k], from_right.at[k], left_send.at[k], left_recv.at[k], (z - 1, b, c))

    def result(j, d):
        return remote(part_tx.at[j, peer(d)], part_rx.at[j, d],
                      part_send.at[j, d], part_recv.at[j, d], (z, peer(d), c))

    def strip_and_piece(k):
        first = k < early
        j = jnp.where(first, k // 2, (k - early) // later)
        p = jnp.where(first, lax.rem(k, 2), 2 + lax.rem(k - early + later * strips, later))
        return j, p

    def produce(k):
        j, p = strip_and_piece(k)
        own[k] = jnp.dot(cols_t[j], feats[p], preferred_element_type=jnp.float32)

    def up(k):
        @pl.when(has_left)
        def _():
            rightward(k).wait_recv()

        @pl.when(has_right)
        def _():
            @pl.when(has_left)
            def _():
                right_tx[k] = (own[k] + from_left[k].astype(jnp.float32)).astype(jnp.bfloat16)

            @pl.when(jnp.logical_not(has_left))
            def _():
                right_tx[k] = own[k].astype(jnp.bfloat16)
            rightward(k).start()

    def down(k):
        @pl.when(has_right)
        def _():
            leftward(k).wait_recv()

        @pl.when(has_left)
        def _():
            @pl.when(has_right)
            def _():
                left_tx[k] = (own[k] + from_right[k].astype(jnp.float32)).astype(jnp.bfloat16)

            @pl.when(jnp.logical_not(has_right))
            def _():
                left_tx[k] = own[k].astype(jnp.bfloat16)
            leftward(k).start()

    def across(left, right):
        return lax.dot_general(left, right, (((1,), (1,)), ((), ())), preferred_element_type=jnp.float32)

    def finish(k):
        j, p = strip_and_piece(k)

        @pl.when(has_left)
        def _():
            own[k] = own[k] + from_left[k].astype(jnp.float32)

        @pl.when(has_right)
        def _():
            own[k] = own[k] + from_right[k].astype(jnp.float32)
        value = across(feats[p], own[k].astype(jnp.bfloat16))
        last = p == pieces - 1

        @pl.when(p == 0)
        def _():
            acc[j] = value

        @pl.when(jnp.logical_and(p > 0, jnp.logical_not(last)))
        def _():
            acc[j] = acc[j] + value

        @pl.when(last)
        def _():
            total = value * (1.0 / dup) - acc[j]
            for q in range(reps):
                part_tx[j, q] = total[q * rows:(q + 1) * rows].astype(jnp.bfloat16)

                @pl.when(b == q)
                def _():
                    part_own[j] = total[q * rows:(q + 1) * rows]
            for d in range(1, reps):
                result(j, d).start()

    lag_up = LAG * z
    lag_down = LAG * (loops - 1 - z)
    lag_end = jnp.maximum(lag_up, lag_down)

    def chunk_at(i):
        k = jnp.where(i < early, i, i - IDLE)
        idle = jnp.logical_and(i >= early, i < early + IDLE)
        return k, jnp.logical_and(jnp.logical_not(idle), jnp.logical_and(i >= 0, k < steps))

    def tick(i, carry):
        for lag, act in ((lag_up, up), (lag_down, down), (lag_end, finish)):
            k, live = chunk_at(i - lag)

            @pl.when(live)
            def _():
                act(k)
        return carry

    def make(k, carry):
        produce(k)
        return tick(jnp.where(k < early, k, k + IDLE), carry)

    def pieces_in(p):
        for d in range(1, reps):
            piece_to(d, p).wait_recv()
            piece_over(d, p).start()

    for p in range(t_own):
        piece_over(0, p).start()
    block_over(0).start()
    strip_in(0)
    turn(0)
    pieces_in(0)
    send_strip(2)
    make(0, 0)
    for d in range(reps):
        piece_over(d, 0).wait_recv()
    make(1, 0)
    for j in range(1, strips):
        strip_in(j)
        send_strip(j + 2)
        if j == min(2, strips - 1):
            for p in range(1, t_own):
                send_piece(p)
        turn(j)
        lax.fori_loop(2 * j, 2 * j + 2, make, 0)
    for d in range(1, reps):
        block_over(d).start()
    feats[pieces - 1, :, :LANES] = cols_all[:, lanes(block)]
    lax.fori_loop(early, early + IDLE, tick, 0)
    for p in range(1, t_own):
        pieces_in(p)
    for d in range(reps):
        for p in range(1, t_own):
            piece_over(d, p).wait_recv()
        block_over(d).wait_recv()
    lax.fori_loop(early, steps, make, 0)
    lax.fori_loop(steps + IDLE, steps + IDLE + LAG * (loops - 1), tick, 0)

    norm = cols_all[mine, :].astype(jnp.float32)
    inner = jnp.zeros((rows, 1), jnp.float32)
    grads = []
    for j in range(strips):
        grad = part_own[j]
        for d in range(1, reps):
            result(j, d).wait_recv()
            grad = grad + part_rx[j, d].astype(jnp.float32)
        grad = grad * coef
        grads.append(grad)
        inner = inner + jnp.sum(grad * norm[:, j * LANES:(j + 1) * LANES], axis=1, keepdims=True)
    inner_tx[...] = jnp.broadcast_to(inner, (rows, LANES))
    swap = remote(inner_tx, inner_rx, inner_sem.at[0], inner_sem.at[1], sibling)
    swap.start()
    swap.wait_recv()
    inner_all = inner_tx[...] + inner_rx[...]
    for j in range(strips):
        at = slice(j * LANES, (j + 1) * LANES)
        out_ref[:, at] = (grads[j] - inner_all * norm[:, at]) * inv_keep[...]

    swap.wait_send()
    for d in range(reps):
        for p in range(t_own):
            piece_over(d, p).wait_send()
            if d:
                piece_to(d, p).wait_send()
        block_over(d).wait_send()
    for j in range(strips):
        for d in range(1, reps):
            strip_to(d, j).wait_send()
            result(j, d).wait_send()

    def drain(k, carry):
        @pl.when(has_right)
        def _():
            rightward(k).wait_send()

        @pl.when(has_left)
        def _():
            leftward(k).wait_send()
        return carry

    lax.fori_loop(0, steps, drain, 0)


def body(loops, reps, student, teacher):
    rows, width = student.shape
    passages = rows * reps * loops
    coef = 32.0 * (2 * width) / math.sqrt(passages)
    dup = max(1, reps * LANES // width)
    t_own = teacher.shape[1] // (reps * PIECE)
    pieces = 1 + 2 * t_own
    strips = width // LANES
    steps = strips * pieces
    total = rows * reps
    f32, bf16 = jnp.float32, jnp.bfloat16
    dma = pltpu.SemaphoreType.DMA
    flops = 4 * total * pieces * PIECE * width
    return pl.pallas_call(
        functools.partial(kernel, loops, reps, coef, dup),
        out_shape=jax.ShapeDtypeStruct((rows, width), f32),
        in_specs=[pl.BlockSpec(memory_space=pltpu.HBM)] * 2,
        out_specs=pl.BlockSpec(memory_space=pltpu.VMEM),
        scratch_shapes=[
            pltpu.VMEM((rows, width), bf16),
            pltpu.VMEM((rows, teacher.shape[1]), bf16),
            pltpu.VMEM((rows, LANES), f32),
            pltpu.VMEM((rows, LANES), f32),
            pltpu.VMEM((rows, LANES), f32),
            pltpu.VMEM((total, width), bf16),
            pltpu.VMEM((strips, LANES, total), bf16),
            pltpu.VMEM((pieces, total, PIECE), bf16),
            pltpu.VMEM((reps, t_own, rows, PIECE), bf16),
            pltpu.VMEM((steps, LANES, PIECE), f32),
            pltpu.VMEM((steps, LANES, PIECE), bf16),
            pltpu.VMEM((steps, LANES, PIECE), bf16),
            pltpu.VMEM((steps, LANES, PIECE), bf16),
            pltpu.VMEM((steps, LANES, PIECE), bf16),
            pltpu.VMEM((strips, total, LANES), f32),
            pltpu.VMEM((strips, reps, rows, LANES), bf16),
            pltpu.VMEM((strips, reps, rows, LANES), bf16),
            pltpu.VMEM((strips, rows, LANES), f32),
            pltpu.VMEM((rows, LANES), f32),
            pltpu.VMEM((rows, LANES), f32),
            dma((2,)),
            dma((2,)),
            dma((strips, reps)),
            dma((strips, reps)),
            dma((t_own, reps)),
            dma((t_own, reps)),
            dma((t_own + 1, reps)),
            dma((t_own + 1, reps)),
            dma((steps,)),
            dma((steps,)),
            dma((steps,)),
            dma((steps,)),
            dma((strips, reps)),
            dma((strips, reps)),
            dma((2,)),
        ],
        compiler_params=pltpu.CompilerParams(
            collective_id=0, has_side_effects=True, vmem_limit_bytes=48 * 1024 * 1024
        ),
        cost_estimate=pl.CostEstimate(flops=flops, bytes_accessed=4 * rows * width, transcendentals=0),
    )(student, teacher)


def solution(mesh):
    placed = P(("loop", "rep"), "sec")
    return jax.shard_map(
        functools.partial(body, mesh.shape["loop"], mesh.shape["rep"]),
        mesh=mesh, in_specs=(placed, placed), out_specs=placed, check_vma=False,
    )
```

```python
import functools
import math

import jax
import jax.numpy as jnp
from jax import lax
from jax.experimental import pallas as pl
from jax.experimental.pallas import tpu as pltpu
from jax.sharding import PartitionSpec as P

MESH = pl.DeviceIdType.MESH
LANES = 128
PIECE = 256
STRIP = 256
HALF = 128
LAG = 3
IDLE = 4
EPS = 1e-6


def kernel(
    loops, reps, coef, dup, s_hbm, t_hbm, out_ref,
    s_ref, t_ref, stat_tx, stat_rx, inv_keep, cols_all, cols_t, feats, feats_tx, own, right_tx, left_tx,
    from_left, from_right, acc, part_tx, part_rx, part_own, inner_tx, inner_rx, whole,
    load_sem, stat_sem, strip_send, strip_recv, gather_send, gather_recv, swap_send, swap_recv,
    right_send, right_recv, left_send, left_recv, part_send, part_recv, inner_sem,
):
    z = lax.axis_index("loop")
    b = lax.axis_index("rep")
    c = lax.axis_index("sec")
    rows, width = s_ref.shape
    pieces, total_rows, _ = feats.shape
    t_own = (pieces - 1) // 2
    strips = width // STRIP
    steps = strips * pieces
    ticks = 2 * steps
    sibling = (z, b, 1 - c)
    has_left = z > 0
    has_right = z < loops - 1

    def peer(d):
        return lax.rem(b + d, reps)

    def span(q):
        return pl.ds(pl.multiple_of(q * rows, rows), rows)

    def lanes(j):
        return pl.ds(pl.multiple_of(j * LANES, LANES), LANES)

    load_s = pltpu.make_async_copy(s_hbm, s_ref, load_sem.at[0])
    load_t = pltpu.make_async_copy(t_hbm, t_ref, load_sem.at[1])
    load_s.start()
    load_t.start()
    barrier = pltpu.get_barrier_semaphore()
    for d in range(1, reps):
        pl.semaphore_signal(barrier, inc=1, device_id=(z, peer(d), c), device_id_type=MESH)
    pl.semaphore_signal(barrier, inc=1, device_id=sibling, device_id_type=MESH)

    @pl.when(has_left)
    def _():
        pl.semaphore_signal(barrier, inc=1, device_id=(z - 1, b, c), device_id_type=MESH)

    @pl.when(has_right)
    def _():
        pl.semaphore_signal(barrier, inc=1, device_id=(z + 1, b, c), device_id_type=MESH)

    load_s.wait()
    s32 = s_ref[...].astype(jnp.float32)
    part_s = jnp.sum(s32 * s32, axis=1, keepdims=True)
    load_t.wait()
    t32 = t_ref[...].astype(jnp.float32)
    part_t = jnp.sum(t32 * t32, axis=1, keepdims=True)
    lane = lax.broadcasted_iota(jnp.int32, (rows, LANES), 1)
    stat_tx[...] = jnp.where(lane < LANES // 2, part_s, part_t)

    pl.semaphore_wait(barrier, reps + has_left.astype(jnp.int32) + has_right.astype(jnp.int32))

    def remote(src, dst, send, recv, device):
        return pltpu.make_async_remote_copy(
            src_ref=src, dst_ref=dst, send_sem=send, recv_sem=recv,
            device_id=device, device_id_type=MESH,
        )

    stat = remote(stat_tx, stat_rx, stat_sem.at[0], stat_sem.at[1], sibling)
    stat.start()
    stat.wait()
    inv = lax.rsqrt(stat_tx[...] + stat_rx[...] + EPS)
    inv_s = inv[:, :1]
    inv_t = inv[:, LANES - 1:]
    inv_keep[...] = jnp.broadcast_to(inv_s, (rows, LANES))
    mine = span(b)
    cols_all[mine, :] = (s_ref[...].astype(jnp.float32) * inv_s).astype(jnp.bfloat16)

    def strip_to(d, j):
        at = slice(j * STRIP, (j + 1) * STRIP)
        return remote(cols_all.at[mine, at], cols_all.at[mine, at],
                      strip_send.at[j, d], strip_recv.at[j, d], (z, peer(d), c))

    def piece_to(d, p):
        return remote(feats_tx.at[peer(d), p], feats.at[2 * p, mine],
                      gather_send.at[p, d], gather_recv.at[p, d], (z, peer(d), c))

    for d in range(1, reps):
        strip_to(d, 0).start()
    for p in range(t_own):
        for q in range(reps):
            lo = (q * t_own + p) * PIECE
            feats_tx[q, p] = (t_ref[:, lo:lo + PIECE].astype(jnp.float32) * inv_t).astype(jnp.bfloat16)
        for d in range(1, reps):
            piece_to(d, p).start()
        feats[2 * p, mine, :] = feats_tx[b, p]
    for j in range(1, strips):
        for d in range(1, reps):
            strip_to(d, j).start()

    block = b // dup

    def came(d):
        return span(lax.rem(b - d + reps, reps))

    def piece_over(d, p):
        at = came(d)
        return remote(feats.at[2 * p, at], feats.at[2 * p + 1, at],
                      swap_send.at[p, d], swap_recv.at[p, d], sibling)

    def block_over(d):
        at = came(d)
        return remote(cols_all.at[at, lanes(block)], feats.at[pieces - 1, at, pl.ds(LANES, LANES)],
                      swap_send.at[t_own, d], swap_recv.at[t_own, d], sibling)

    def strip_in(j):
        for d in range(1, reps):
            strip_to(d, j).wait_recv()

    def turn(j):
        cols_t[j] = cols_all[:, j * STRIP:(j + 1) * STRIP].T

    def rightward(k):
        return remote(right_tx.at[k], from_left.at[k], right_send.at[k], right_recv.at[k], (z + 1, b, c))

    def leftward(k):
        return remote(left_tx.at[k], from_right.at[k], left_send.at[k], left_recv.at[k], (z - 1, b, c))

    def result(j, d):
        return remote(part_tx.at[j, peer(d)], part_rx.at[j, d],
                      part_send.at[j, d], part_recv.at[j, d], (z, peer(d), c))

    def produce(k):
        value = jnp.dot(
            cols_t[k // pieces], feats[lax.rem(k, pieces)], preferred_element_type=jnp.float32
        )
        own[2 * k] = value[:HALF]
        own[2 * k + 1] = value[HALF:]

    def up(k):
        @pl.when(has_left)
        def _():
            rightward(k).wait_recv()

        @pl.when(has_right)
        def _():
            @pl.when(has_left)
            def _():
                right_tx[k] = (own[k] + from_left[k].astype(jnp.float32)).astype(jnp.bfloat16)

            @pl.when(jnp.logical_not(has_left))
            def _():
                right_tx[k] = own[k].astype(jnp.bfloat16)
            rightward(k).start()

    def down(k):
        @pl.when(has_right)
        def _():
            leftward(k).wait_recv()

        @pl.when(has_left)
        def _():
            @pl.when(has_right)
            def _():
                left_tx[k] = (own[k] + from_right[k].astype(jnp.float32)).astype(jnp.bfloat16)

            @pl.when(jnp.logical_not(has_right))
            def _():
                left_tx[k] = own[k].astype(jnp.bfloat16)
            leftward(k).start()

    def across(left, right):
        return lax.dot_general(left, right, (((1,), (1,)), ((), ())), preferred_element_type=jnp.float32)

    def finish(k):
        j = k // pieces
        p = lax.rem(k, pieces)
        both = pl.ds(2 * k, 2)

        def joined(ref):
            return ref[both].reshape(STRIP, PIECE).astype(jnp.float32)

        @pl.when(jnp.logical_and(has_left, has_right))
        def _():
            whole[...] = (joined(own) + joined(from_left) + joined(from_right)).astype(jnp.bfloat16)

        @pl.when(jnp.logical_not(has_left))
        def _():
            whole[...] = (joined(own) + joined(from_right)).astype(jnp.bfloat16)

        @pl.when(jnp.logical_not(has_right))
        def _():
            whole[...] = (joined(own) + joined(from_left)).astype(jnp.bfloat16)
        value = across(feats[p], whole[...])
        last = p == pieces - 1

        @pl.when(p == 0)
        def _():
            acc[...] = value

        @pl.when(jnp.logical_and(p > 0, jnp.logical_not(last)))
        def _():
            acc[...] = acc[...] + value

        @pl.when(last)
        def _():
            total = value * (1.0 / dup) - acc[...]
            for q in range(reps):
                part_tx[j, q] = total[q * rows:(q + 1) * rows].astype(jnp.bfloat16)

                @pl.when(b == q)
                def _():
                    part_own[j] = total[q * rows:(q + 1) * rows]
            for d in range(1, reps):
                result(j, d).start()

    lag_up = LAG * z
    lag_down = LAG * (loops - 1 - z)
    lag_end = jnp.maximum(lag_up, lag_down)
    early = 4

    def half_at(i):
        h = jnp.where(i < early, i, i - IDLE)
        idle = jnp.logical_and(i >= early, i < early + IDLE)
        return h, jnp.logical_and(jnp.logical_not(idle), jnp.logical_and(i >= 0, h < ticks))

    def tick(i, carry):
        for lag, act in ((lag_up, up), (lag_down, down)):
            h, live = half_at(i - lag)

            @pl.when(live)
            def _():
                act(h)
        h, live = half_at(i - lag_end)

        @pl.when(jnp.logical_and(live, lax.rem(h, 2) == 1))
        def _():
            finish(h // 2)
        return carry

    def make(k, carry):
        produce(k)
        first = 2 * k if isinstance(k, int) and k < 2 else 2 * k + IDLE
        return lax.fori_loop(first, first + 2, tick, carry)

    for p in range(t_own):
        piece_over(0, p).start()
    block_over(0).start()
    strip_in(0)
    turn(0)
    for p in range(t_own):
        for d in range(1, reps):
            piece_to(d, p).wait_recv()
            piece_over(d, p).start()
        make(2 * p, 0)
        for d in range(reps):
            piece_over(d, p).wait_recv()
        make(2 * p + 1, 0)
        if p == 0:
            lax.fori_loop(early, early + IDLE, tick, 0)
    for j in range(1, strips):
        strip_in(j)
    for d in range(1, reps):
        block_over(d).start()
    feats[pieces - 1, :, :LANES] = cols_all[:, lanes(block)]
    for j in range(1, strips):
        turn(j)
    for d in range(reps):
        block_over(d).wait_recv()
    lax.fori_loop(pieces - 1, steps, make, 0)
    lax.fori_loop(ticks + IDLE, ticks + IDLE + LAG * (loops - 1), tick, 0)

    norm = cols_all[mine, :].astype(jnp.float32)
    inner = jnp.zeros((rows, 1), jnp.float32)
    grads = []
    for j in range(strips):
        grad = part_own[j]
        for d in range(1, reps):
            result(j, d).wait_recv()
            grad = grad + part_rx[j, d].astype(jnp.float32)
        grad = grad * coef
        grads.append(grad)
        inner = inner + jnp.sum(grad * norm[:, j * STRIP:(j + 1) * STRIP], axis=1, keepdims=True)
    inner_tx[...] = jnp.broadcast_to(inner, (rows, LANES))
    swap = remote(inner_tx, inner_rx, inner_sem.at[0], inner_sem.at[1], sibling)
    swap.start()
    swap.wait_recv()
    inner_all = (inner_tx[...] + inner_rx[...])[:, :1]
    scale = inv_keep[...][:, :1]
    for j in range(strips):
        at = slice(j * STRIP, (j + 1) * STRIP)
        out_ref[:, at] = (grads[j] - inner_all * norm[:, at]) * scale

    swap.wait_send()
    for d in range(reps):
        for p in range(t_own):
            piece_over(d, p).wait_send()
            if d:
                piece_to(d, p).wait_send()
        block_over(d).wait_send()
    for j in range(strips):
        for d in range(1, reps):
            strip_to(d, j).wait_send()
            result(j, d).wait_send()

    def drain(k, carry):
        @pl.when(has_right)
        def _():
            rightward(k).wait_send()

        @pl.when(has_left)
        def _():
            leftward(k).wait_send()
        return carry

    lax.fori_loop(0, ticks, drain, 0)


def body(loops, reps, student, teacher):
    rows, width = student.shape
    passages = rows * reps * loops
    coef = 32.0 * (2 * width) / math.sqrt(passages)
    dup = max(1, reps * LANES // width)
    t_own = teacher.shape[1] // (reps * PIECE)
    pieces = 1 + 2 * t_own
    strips = width // STRIP
    ticks = 2 * strips * pieces
    total = rows * reps
    f32, bf16 = jnp.float32, jnp.bfloat16
    dma = pltpu.SemaphoreType.DMA
    flops = 4 * total * pieces * PIECE * width
    return pl.pallas_call(
        functools.partial(kernel, loops, reps, coef, dup),
        out_shape=jax.ShapeDtypeStruct((rows, width), f32),
        in_specs=[pl.BlockSpec(memory_space=pltpu.HBM)] * 2,
        out_specs=pl.BlockSpec(memory_space=pltpu.VMEM),
        scratch_shapes=[
            pltpu.VMEM((rows, width), bf16),
            pltpu.VMEM((rows, teacher.shape[1]), bf16),
            pltpu.VMEM((rows, LANES), f32),
            pltpu.VMEM((rows, LANES), f32),
            pltpu.VMEM((rows, LANES), f32),
            pltpu.VMEM((total, width), bf16),
            pltpu.VMEM((strips, STRIP, total), bf16),
            pltpu.VMEM((pieces, total, PIECE), bf16),
            pltpu.VMEM((reps, t_own, rows, PIECE), bf16),
            pltpu.VMEM((ticks, HALF, PIECE), f32),
            pltpu.VMEM((ticks, HALF, PIECE), bf16),
            pltpu.VMEM((ticks, HALF, PIECE), bf16),
            pltpu.VMEM((ticks, HALF, PIECE), bf16),
            pltpu.VMEM((ticks, HALF, PIECE), bf16),
            pltpu.VMEM((total, STRIP), f32),
            pltpu.VMEM((strips, reps, rows, STRIP), bf16),
            pltpu.VMEM((strips, reps, rows, STRIP), bf16),
            pltpu.VMEM((strips, rows, STRIP), f32),
            pltpu.VMEM((rows, LANES), f32),
            pltpu.VMEM((rows, LANES), f32),
            pltpu.VMEM((STRIP, PIECE), bf16),
            dma((2,)),
            dma((2,)),
            dma((strips, reps)),
            dma((strips, reps)),
            dma((t_own, reps)),
            dma((t_own, reps)),
            dma((t_own + 1, reps)),
            dma((t_own + 1, reps)),
            dma((ticks,)),
            dma((ticks,)),
            dma((ticks,)),
            dma((ticks,)),
            dma((strips, reps)),
            dma((strips, reps)),
            dma((2,)),
        ],
        compiler_params=pltpu.CompilerParams(
            collective_id=0, has_side_effects=True, vmem_limit_bytes=48 * 1024 * 1024
        ),
        cost_estimate=pl.CostEstimate(flops=flops, bytes_accessed=4 * rows * width, transcendentals=0),
    )(student, teacher)


def solution(mesh):
    placed = P(("loop", "rep"), "sec")
    return jax.shard_map(
        functools.partial(body, mesh.shape["loop"], mesh.shape["rep"]),
        mesh=mesh, in_specs=(placed, placed), out_specs=placed, check_vma=False,
    )
```

```python
import functools
import math

import jax
import jax.numpy as jnp
from jax import lax
from jax.experimental import pallas as pl
from jax.experimental.pallas import tpu as pltpu
from jax.sharding import PartitionSpec as P

MESH = pl.DeviceIdType.MESH
LANES = 128
PIECE = 256
LAG = 3
IDLE = 3
EPS = 1e-6


def kernel(
    loops, reps, coef, dup, s_hbm, t_hbm, out_ref,
    s_ref, t_ref, stat_tx, stat_rx, inv_keep, cols_all, cols_t, feats, feats_tx, own, right_tx, left_tx,
    from_left, from_right, full, part_tx, part_rx, part_own, inner_tx, inner_rx,
    load_sem, stat_sem, strip_send, strip_recv, gather_send, gather_recv, swap_send, swap_recv,
    right_send, right_recv, left_send, left_recv, part_send, part_recv, inner_sem,
):
    z = lax.axis_index("loop")
    b = lax.axis_index("rep")
    c = lax.axis_index("sec")
    rows, width = s_ref.shape
    pieces, total_rows, _ = feats.shape
    t_own = (pieces - 1) // 2
    strips = width // LANES
    steps = strips * pieces
    early = 2 * strips
    later = pieces - 2
    sibling = (z, b, 1 - c)
    has_left = z > 0
    has_right = z < loops - 1

    def peer(d):
        return lax.rem(b + d, reps)

    def span(q):
        return pl.ds(pl.multiple_of(q * rows, rows), rows)

    def lanes(j):
        return pl.ds(pl.multiple_of(j * LANES, LANES), LANES)

    load_s = pltpu.make_async_copy(s_hbm, s_ref, load_sem.at[0])
    load_t = pltpu.make_async_copy(t_hbm, t_ref, load_sem.at[1])
    load_s.start()
    load_t.start()
    barrier = pltpu.get_barrier_semaphore()
    for d in range(1, reps):
        pl.semaphore_signal(barrier, inc=1, device_id=(z, peer(d), c), device_id_type=MESH)
    pl.semaphore_signal(barrier, inc=1, device_id=sibling, device_id_type=MESH)

    @pl.when(has_left)
    def _():
        pl.semaphore_signal(barrier, inc=1, device_id=(z - 1, b, c), device_id_type=MESH)

    @pl.when(has_right)
    def _():
        pl.semaphore_signal(barrier, inc=1, device_id=(z + 1, b, c), device_id_type=MESH)

    load_s.wait()
    s32 = s_ref[...].astype(jnp.float32)
    part_s = jnp.sum(s32 * s32, axis=1, keepdims=True)
    load_t.wait()
    t32 = t_ref[...].astype(jnp.float32)
    part_t = jnp.sum(t32 * t32, axis=1, keepdims=True)
    lane = lax.broadcasted_iota(jnp.int32, (rows, LANES), 1)
    stat_tx[...] = jnp.where(lane < LANES // 2, part_s, part_t)

    pl.semaphore_wait(barrier, reps + has_left.astype(jnp.int32) + has_right.astype(jnp.int32))

    def remote(src, dst, send, recv, device):
        return pltpu.make_async_remote_copy(
            src_ref=src, dst_ref=dst, send_sem=send, recv_sem=recv,
            device_id=device, device_id_type=MESH,
        )

    stat = remote(stat_tx, stat_rx, stat_sem.at[0], stat_sem.at[1], sibling)
    stat.start()
    stat.wait()
    inv = lax.rsqrt(stat_tx[...] + stat_rx[...] + EPS)
    inv_s = inv[:, :1]
    inv_t = inv[:, LANES - 1:]
    inv_keep[...] = jnp.broadcast_to(inv_s, (rows, LANES))
    mine = span(b)
    cols_all[mine, :] = (s_ref[...].astype(jnp.float32) * inv_s).astype(jnp.bfloat16)

    def strip_to(d, j):
        at = lanes(j)
        return remote(cols_all.at[mine, at], cols_all.at[mine, at],
                      strip_send.at[j, d], strip_recv.at[j, d], (z, peer(d), c))

    def piece_to(d, p):
        return remote(feats_tx.at[peer(d), p], feats.at[2 * p, mine],
                      gather_send.at[p, d], gather_recv.at[p, d], (z, peer(d), c))

    def send_strip(j):
        if j < strips:
            for d in range(1, reps):
                strip_to(d, j).start()

    def send_piece(p):
        for d in range(1, reps):
            piece_to(d, p).start()

    send_strip(0)
    for p in range(t_own):
        for q in range(reps):
            lo = (q * t_own + p) * PIECE
            feats_tx[q, p] = (t_ref[:, lo:lo + PIECE].astype(jnp.float32) * inv_t).astype(jnp.bfloat16)
        if p == 0:
            send_piece(0)
            send_strip(1)
        feats[2 * p, mine, :] = feats_tx[b, p]

    block = b // dup

    def came(d):
        return span(lax.rem(b - d + reps, reps))

    def piece_over(d, p):
        at = came(d)
        return remote(feats.at[2 * p, at], feats.at[2 * p + 1, at],
                      swap_send.at[p, d], swap_recv.at[p, d], sibling)

    def block_over(d):
        at = came(d)
        return remote(cols_all.at[at, lanes(block)], feats.at[pieces - 1, at, pl.ds(LANES, LANES)],
                      swap_send.at[t_own, d], swap_recv.at[t_own, d], sibling)

    def strip_in(j):
        for d in range(1, reps):
            strip_to(d, j).wait_recv()

    def turn(j):
        cols_t[j] = cols_all[:, j * LANES:(j + 1) * LANES].T

    def rightward(k):
        return remote(right_tx.at[k], from_left.at[k], right_send.at[k], right_recv.at[k], (z + 1, b, c))

    def leftward(k):
        return remote(left_tx.at[k], from_right.at[k], left_send.at[k], left_recv.at[k], (z - 1, b, c))

    def result(j, d):
        return remote(part_tx.at[j, peer(d)], part_rx.at[j, d],
                      part_send.at[j, d], part_recv.at[j, d], (z, peer(d), c))

    def strip_and_piece(k):
        first = k < early
        j = jnp.where(first, k // 2, (k - early) // later)
        p = jnp.where(first, lax.rem(k, 2), 2 + lax.rem(k - early + later * strips, later))
        return j, p

    def produce(k):
        j, p = strip_and_piece(k)
        own[k] = jnp.dot(cols_t[j], feats[p], preferred_element_type=jnp.float32)

    def up(k):
        @pl.when(has_left)
        def _():
            rightward(k).wait_recv()

        @pl.when(has_right)
        def _():
            @pl.when(has_left)
            def _():
                right_tx[k] = (own[k] + from_left[k].astype(jnp.float32)).astype(jnp.bfloat16)

            @pl.when(jnp.logical_not(has_left))
            def _():
                right_tx[k] = own[k].astype(jnp.bfloat16)
            rightward(k).start()

    def down(k):
        @pl.when(has_right)
        def _():
            leftward(k).wait_recv()

        @pl.when(has_left)
        def _():
            @pl.when(has_right)
            def _():
                left_tx[k] = (own[k] + from_right[k].astype(jnp.float32)).astype(jnp.bfloat16)

            @pl.when(jnp.logical_not(has_right))
            def _():
                left_tx[k] = own[k].astype(jnp.bfloat16)
            leftward(k).start()

    def across(left, right):
        return lax.dot_general(left, right, (((1,), (1,)), ((), ())), preferred_element_type=jnp.float32)

    def finish(k):
        j, p = strip_and_piece(k)

        last = p == pieces - 1
        sign = jnp.where(last, 1.0 / dup, -1.0)

        @pl.when(jnp.logical_and(has_left, has_right))
        def _():
            total = own[k] + from_left[k].astype(jnp.float32) + from_right[k].astype(jnp.float32)
            full[j, p] = (total * sign).astype(jnp.bfloat16)

        @pl.when(jnp.logical_not(has_left))
        def _():
            full[j, p] = ((own[k] + from_right[k].astype(jnp.float32)) * sign).astype(jnp.bfloat16)

        @pl.when(jnp.logical_not(has_right))
        def _():
            full[j, p] = ((own[k] + from_left[k].astype(jnp.float32)) * sign).astype(jnp.bfloat16)

        @pl.when(last)
        def _():
            total = across(
                jnp.concatenate([feats[q] for q in range(pieces)], axis=1),
                jnp.concatenate([full[j, q] for q in range(pieces)], axis=1),
            )
            for q in range(reps):
                part_tx[j, q] = total[q * rows:(q + 1) * rows].astype(jnp.bfloat16)

                @pl.when(b == q)
                def _():
                    part_own[j] = total[q * rows:(q + 1) * rows]
            for d in range(1, reps):
                result(j, d).start()

    lag_up = LAG * z
    lag_down = LAG * (loops - 1 - z)
    lag_end = jnp.maximum(lag_up, lag_down)

    def chunk_at(i):
        k = jnp.where(i < early, i, i - IDLE)
        idle = jnp.logical_and(i >= early, i < early + IDLE)
        return k, jnp.logical_and(jnp.logical_not(idle), jnp.logical_and(i >= 0, k < steps))

    def tick(i, carry):
        for lag, act in ((lag_up, up), (lag_down, down), (lag_end, finish)):
            k, live = chunk_at(i - lag)

            @pl.when(live)
            def _():
                act(k)
        return carry

    def make(k, carry):
        produce(k)
        return tick(jnp.where(k < early, k, k + IDLE), carry)

    def pieces_in(p):
        for d in range(1, reps):
            piece_to(d, p).wait_recv()
            piece_over(d, p).start()

    for p in range(t_own):
        piece_over(0, p).start()
    block_over(0).start()
    strip_in(0)
    turn(0)
    pieces_in(0)
    send_strip(2)
    make(0, 0)
    for d in range(reps):
        piece_over(d, 0).wait_recv()
    make(1, 0)
    for j in range(1, strips):
        strip_in(j)
        send_strip(j + 2)
        if j == min(2, strips - 1):
            for p in range(1, t_own):
                send_piece(p)
        turn(j)
        lax.fori_loop(2 * j, 2 * j + 2, make, 0)
    for d in range(1, reps):
        block_over(d).start()
    feats[pieces - 1, :, :LANES] = cols_all[:, lanes(block)]
    lax.fori_loop(early, early + IDLE, tick, 0)
    for p in range(1, t_own):
        pieces_in(p)
    for d in range(reps):
        for p in range(1, t_own):
            piece_over(d, p).wait_recv()
        block_over(d).wait_recv()
    lax.fori_loop(early, steps, make, 0)
    lax.fori_loop(steps + IDLE, steps + IDLE + LAG * (loops - 1), tick, 0)

    norm = cols_all[mine, :].astype(jnp.float32)
    inner = jnp.zeros((rows, 1), jnp.float32)
    grads = []
    for j in range(strips):
        grad = part_own[j]
        for d in range(1, reps):
            result(j, d).wait_recv()
            grad = grad + part_rx[j, d].astype(jnp.float32)
        grad = grad * coef
        grads.append(grad)
        inner = inner + jnp.sum(grad * norm[:, j * LANES:(j + 1) * LANES], axis=1, keepdims=True)
    inner_tx[...] = jnp.broadcast_to(inner, (rows, LANES))
    swap = remote(inner_tx, inner_rx, inner_sem.at[0], inner_sem.at[1], sibling)
    swap.start()
    swap.wait_recv()
    inner_all = inner_tx[...] + inner_rx[...]
    for j in range(strips):
        at = slice(j * LANES, (j + 1) * LANES)
        out_ref[:, at] = (grads[j] - inner_all * norm[:, at]) * inv_keep[...]

    swap.wait_send()
    for d in range(reps):
        for p in range(t_own):
            piece_over(d, p).wait_send()
            if d:
                piece_to(d, p).wait_send()
        block_over(d).wait_send()
    for j in range(strips):
        for d in range(1, reps):
            strip_to(d, j).wait_send()
            result(j, d).wait_send()

    def drain(k, carry):
        @pl.when(has_right)
        def _():
            rightward(k).wait_send()

        @pl.when(has_left)
        def _():
            leftward(k).wait_send()
        return carry

    lax.fori_loop(0, steps, drain, 0)


def body(loops, reps, student, teacher):
    rows, width = student.shape
    passages = rows * reps * loops
    coef = 32.0 * (2 * width) / math.sqrt(passages)
    dup = max(1, reps * LANES // width)
    t_own = teacher.shape[1] // (reps * PIECE)
    pieces = 1 + 2 * t_own
    strips = width // LANES
    steps = strips * pieces
    total = rows * reps
    f32, bf16 = jnp.float32, jnp.bfloat16
    dma = pltpu.SemaphoreType.DMA
    flops = 4 * total * pieces * PIECE * width
    return pl.pallas_call(
        functools.partial(kernel, loops, reps, coef, dup),
        out_shape=jax.ShapeDtypeStruct((rows, width), f32),
        in_specs=[pl.BlockSpec(memory_space=pltpu.HBM)] * 2,
        out_specs=pl.BlockSpec(memory_space=pltpu.VMEM),
        scratch_shapes=[
            pltpu.VMEM((rows, width), bf16),
            pltpu.VMEM((rows, teacher.shape[1]), bf16),
            pltpu.VMEM((rows, LANES), f32),
            pltpu.VMEM((rows, LANES), f32),
            pltpu.VMEM((rows, LANES), f32),
            pltpu.VMEM((total, width), bf16),
            pltpu.VMEM((strips, LANES, total), bf16),
            pltpu.VMEM((pieces, total, PIECE), bf16),
            pltpu.VMEM((reps, t_own, rows, PIECE), bf16),
            pltpu.VMEM((steps, LANES, PIECE), f32),
            pltpu.VMEM((steps, LANES, PIECE), bf16),
            pltpu.VMEM((steps, LANES, PIECE), bf16),
            pltpu.VMEM((steps, LANES, PIECE), bf16),
            pltpu.VMEM((steps, LANES, PIECE), bf16),
            pltpu.VMEM((strips, pieces, LANES, PIECE), bf16),
            pltpu.VMEM((strips, reps, rows, LANES), bf16),
            pltpu.VMEM((strips, reps, rows, LANES), bf16),
            pltpu.VMEM((strips, rows, LANES), f32),
            pltpu.VMEM((rows, LANES), f32),
            pltpu.VMEM((rows, LANES), f32),
            dma((2,)),
            dma((2,)),
            dma((strips, reps)),
            dma((strips, reps)),
            dma((t_own, reps)),
            dma((t_own, reps)),
            dma((t_own + 1, reps)),
            dma((t_own + 1, reps)),
            dma((steps,)),
            dma((steps,)),
            dma((steps,)),
            dma((steps,)),
            dma((strips, reps)),
            dma((strips, reps)),
            dma((2,)),
        ],
        compiler_params=pltpu.CompilerParams(
            collective_id=0, has_side_effects=True, vmem_limit_bytes=48 * 1024 * 1024
        ),
        cost_estimate=pl.CostEstimate(flops=flops, bytes_accessed=4 * rows * width, transcendentals=0),
    )(student, teacher)


def solution(mesh):
    placed = P(("loop", "rep"), "sec")
    return jax.shard_map(
        functools.partial(body, mesh.shape["loop"], mesh.shape["rep"]),
        mesh=mesh, in_specs=(placed, placed), out_specs=placed, check_vma=False,
    )
```

```python
import functools
import math

import jax
import jax.numpy as jnp
from jax import lax
from jax.experimental import pallas as pl
from jax.experimental.pallas import tpu as pltpu
from jax.sharding import PartitionSpec as P

MESH = pl.DeviceIdType.MESH
LANES = 128
PIECE = 256
LAG = 2
IDLE = 2
EPS = 1e-6


def kernel(
    loops, reps, coef, dup, s_hbm, t_hbm, out_ref,
    s_ref, t_ref, stat_tx, stat_rx, inv_keep, cols_all, cols_t, feats, feats_tx, own, right_tx, left_tx,
    from_left, from_right, full, part_tx, part_rx, part_own, inner_tx, inner_rx,
    load_sem, stat_sem, strip_send, strip_recv, gather_send, gather_recv, swap_send, swap_recv,
    right_send, right_recv, left_send, left_recv, part_send, part_recv, inner_sem,
):
    z = lax.axis_index("loop")
    b = lax.axis_index("rep")
    c = lax.axis_index("sec")
    rows, width = s_ref.shape
    pieces, total_rows, _ = feats.shape
    t_own = (pieces - 1) // 2
    strips = width // LANES
    steps = strips * pieces
    early = 2 * strips
    later = pieces - 2
    sibling = (z, b, 1 - c)
    has_left = z > 0
    has_right = z < loops - 1

    def peer(d):
        return lax.rem(b + d, reps)

    def span(q):
        return pl.ds(pl.multiple_of(q * rows, rows), rows)

    def lanes(j):
        return pl.ds(pl.multiple_of(j * LANES, LANES), LANES)

    load_s = pltpu.make_async_copy(s_hbm, s_ref, load_sem.at[0])
    load_t = pltpu.make_async_copy(t_hbm, t_ref, load_sem.at[1])
    load_s.start()
    load_t.start()
    barrier = pltpu.get_barrier_semaphore()
    for d in range(1, reps):
        pl.semaphore_signal(barrier, inc=1, device_id=(z, peer(d), c), device_id_type=MESH)
    pl.semaphore_signal(barrier, inc=1, device_id=sibling, device_id_type=MESH)

    @pl.when(has_left)
    def _():
        pl.semaphore_signal(barrier, inc=1, device_id=(z - 1, b, c), device_id_type=MESH)

    @pl.when(has_right)
    def _():
        pl.semaphore_signal(barrier, inc=1, device_id=(z + 1, b, c), device_id_type=MESH)

    load_s.wait()
    s32 = s_ref[...].astype(jnp.float32)
    part_s = jnp.sum(s32 * s32, axis=1, keepdims=True)
    load_t.wait()
    t32 = t_ref[...].astype(jnp.float32)
    part_t = jnp.sum(t32 * t32, axis=1, keepdims=True)
    lane = lax.broadcasted_iota(jnp.int32, (rows, LANES), 1)
    stat_tx[...] = jnp.where(lane < LANES // 2, part_s, part_t)

    pl.semaphore_wait(barrier, reps + has_left.astype(jnp.int32) + has_right.astype(jnp.int32))

    def remote(src, dst, send, recv, device):
        return pltpu.make_async_remote_copy(
            src_ref=src, dst_ref=dst, send_sem=send, recv_sem=recv,
            device_id=device, device_id_type=MESH,
        )

    stat = remote(stat_tx, stat_rx, stat_sem.at[0], stat_sem.at[1], sibling)
    stat.start()
    stat.wait()
    inv = lax.rsqrt(stat_tx[...] + stat_rx[...] + EPS)
    inv_s = inv[:, :1]
    inv_t = inv[:, LANES - 1:]
    inv_keep[...] = jnp.broadcast_to(inv_s, (rows, LANES))
    mine = span(b)
    cols_all[mine, :] = (s_ref[...].astype(jnp.float32) * inv_s).astype(jnp.bfloat16)

    def strip_to(d, j):
        at = lanes(j)
        return remote(cols_all.at[mine, at], cols_all.at[mine, at],
                      strip_send.at[j, d], strip_recv.at[j, d], (z, peer(d), c))

    def piece_to(d, p):
        return remote(feats_tx.at[peer(d), p], feats.at[2 * p, mine],
                      gather_send.at[p, d], gather_recv.at[p, d], (z, peer(d), c))

    def send_strip(j):
        if j < strips:
            for d in range(1, reps):
                strip_to(d, j).start()

    def send_piece(p):
        for d in range(1, reps):
            piece_to(d, p).start()

    send_strip(0)
    for p in range(t_own):
        for q in range(reps):
            lo = (q * t_own + p) * PIECE
            feats_tx[q, p] = (t_ref[:, lo:lo + PIECE].astype(jnp.float32) * inv_t).astype(jnp.bfloat16)
        if p == 0:
            send_piece(0)
            send_strip(1)
        feats[2 * p, mine, :] = feats_tx[b, p]

    block = b // dup

    def came(d):
        return span(lax.rem(b - d + reps, reps))

    def piece_over(d, p):
        at = came(d)
        return remote(feats.at[2 * p, at], feats.at[2 * p + 1, at],
                      swap_send.at[p, d], swap_recv.at[p, d], sibling)

    def block_over(d):
        at = came(d)
        return remote(cols_all.at[at, lanes(block)], feats.at[pieces - 1, at, pl.ds(LANES, LANES)],
                      swap_send.at[t_own, d], swap_recv.at[t_own, d], sibling)

    def strip_in(j):
        for d in range(1, reps):
            strip_to(d, j).wait_recv()

    def turn(j):
        cols_t[j] = cols_all[:, j * LANES:(j + 1) * LANES].T

    def rightward(k):
        return remote(right_tx.at[k], from_left.at[k], right_send.at[k], right_recv.at[k], (z + 1, b, c))

    def leftward(k):
        return remote(left_tx.at[k], from_right.at[k], left_send.at[k], left_recv.at[k], (z - 1, b, c))

    def result(j, d):
        return remote(part_tx.at[j, peer(d)], part_rx.at[j, d],
                      part_send.at[j, d], part_recv.at[j, d], (z, peer(d), c))

    def strip_and_piece(k):
        first = k < early
        j = jnp.where(first, k // 2, (k - early) // later)
        p = jnp.where(first, lax.rem(k, 2), 2 + lax.rem(k - early + later * strips, later))
        return j, p

    def produce(k):
        j, p = strip_and_piece(k)
        own[k] = jnp.dot(cols_t[j], feats[p], preferred_element_type=jnp.float32)

    def up(k):
        @pl.when(has_left)
        def _():
            rightward(k).wait_recv()

        @pl.when(has_right)
        def _():
            @pl.when(has_left)
            def _():
                right_tx[k] = (own[k] + from_left[k].astype(jnp.float32)).astype(jnp.bfloat16)

            @pl.when(jnp.logical_not(has_left))
            def _():
                right_tx[k] = own[k].astype(jnp.bfloat16)
            rightward(k).start()

    def down(k):
        @pl.when(has_right)
        def _():
            leftward(k).wait_recv()

        @pl.when(has_left)
        def _():
            @pl.when(has_right)
            def _():
                left_tx[k] = (own[k] + from_right[k].astype(jnp.float32)).astype(jnp.bfloat16)

            @pl.when(jnp.logical_not(has_right))
            def _():
                left_tx[k] = own[k].astype(jnp.bfloat16)
            leftward(k).start()

    def across(left, right):
        return lax.dot_general(left, right, (((1,), (1,)), ((), ())), preferred_element_type=jnp.float32)

    def finish(k):
        j, p = strip_and_piece(k)

        last = p == pieces - 1
        sign = jnp.where(last, 1.0 / dup, -1.0)

        @pl.when(jnp.logical_and(has_left, has_right))
        def _():
            total = own[k] + from_left[k].astype(jnp.float32) + from_right[k].astype(jnp.float32)
            full[j, p] = (total * sign).astype(jnp.bfloat16)

        @pl.when(jnp.logical_not(has_left))
        def _():
            full[j, p] = ((own[k] + from_right[k].astype(jnp.float32)) * sign).astype(jnp.bfloat16)

        @pl.when(jnp.logical_not(has_right))
        def _():
            full[j, p] = ((own[k] + from_left[k].astype(jnp.float32)) * sign).astype(jnp.bfloat16)

        @pl.when(last)
        def _():
            total = across(
                jnp.concatenate([feats[q] for q in range(pieces)], axis=1),
                jnp.concatenate([full[j, q] for q in range(pieces)], axis=1),
            )
            for q in range(reps):
                part_tx[j, q] = total[q * rows:(q + 1) * rows].astype(jnp.bfloat16)

                @pl.when(b == q)
                def _():
                    part_own[j] = total[q * rows:(q + 1) * rows]
            for d in range(1, reps):
                result(j, d).start()

    lag_up = LAG * z
    lag_down = LAG * (loops - 1 - z)
    lag_end = jnp.maximum(lag_up, lag_down)

    def chunk_at(i):
        k = jnp.where(i < early, i, i - IDLE)
        idle = jnp.logical_and(i >= early, i < early + IDLE)
        return k, jnp.logical_and(jnp.logical_not(idle), jnp.logical_and(i >= 0, k < steps))

    def tick(i, carry):
        for lag, act in ((lag_up, up), (lag_down, down), (lag_end, finish)):
            k, live = chunk_at(i - lag)

            @pl.when(live)
            def _():
                act(k)
        return carry

    def make(k, carry):
        produce(k)
        return tick(jnp.where(k < early, k, k + IDLE), carry)

    def pieces_in(p):
        for d in range(1, reps):
            piece_to(d, p).wait_recv()
            piece_over(d, p).start()

    for p in range(t_own):
        piece_over(0, p).start()
    block_over(0).start()
    strip_in(0)
    turn(0)
    pieces_in(0)
    send_strip(2)
    make(0, 0)
    for d in range(reps):
        piece_over(d, 0).wait_recv()
    make(1, 0)
    for j in range(1, strips):
        strip_in(j)
        send_strip(j + 2)
        if j == min(2, strips - 1):
            for p in range(1, t_own):
                send_piece(p)
        turn(j)
        lax.fori_loop(2 * j, 2 * j + 2, make, 0)
    for d in range(1, reps):
        block_over(d).start()
    feats[pieces - 1, :, :LANES] = cols_all[:, lanes(block)]
    lax.fori_loop(early, early + IDLE, tick, 0)
    for p in range(1, t_own):
        pieces_in(p)
    for d in range(reps):
        for p in range(1, t_own):
            piece_over(d, p).wait_recv()
        block_over(d).wait_recv()
    lax.fori_loop(early, steps, make, 0)
    lax.fori_loop(steps + IDLE, steps + IDLE + LAG * (loops - 1), tick, 0)

    norm = cols_all[mine, :].astype(jnp.float32)
    inner = jnp.zeros((rows, 1), jnp.float32)
    grads = []
    for j in range(strips):
        grad = part_own[j]
        for d in range(1, reps):
            result(j, d).wait_recv()
            grad = grad + part_rx[j, d].astype(jnp.float32)
        grad = grad * coef
        grads.append(grad)
        inner = inner + jnp.sum(grad * norm[:, j * LANES:(j + 1) * LANES], axis=1, keepdims=True)
    inner_tx[...] = jnp.broadcast_to(inner, (rows, LANES))
    swap = remote(inner_tx, inner_rx, inner_sem.at[0], inner_sem.at[1], sibling)
    swap.start()
    for d in range(reps):
        for p in range(t_own):
            piece_over(d, p).wait_send()
            if d:
                piece_to(d, p).wait_send()
        block_over(d).wait_send()
    for j in range(strips):
        for d in range(1, reps):
            strip_to(d, j).wait_send()
            result(j, d).wait_send()

    def drain(k, carry):
        @pl.when(has_right)
        def _():
            rightward(k).wait_send()

        @pl.when(has_left)
        def _():
            leftward(k).wait_send()
        return carry

    lax.fori_loop(0, steps, drain, 0)

    swap.wait_recv()
    inner_all = inner_tx[...] + inner_rx[...]
    for j in range(strips):
        at = slice(j * LANES, (j + 1) * LANES)
        out_ref[:, at] = (grads[j] - inner_all * norm[:, at]) * inv_keep[...]

    swap.wait_send()


def body(loops, reps, student, teacher):
    rows, width = student.shape
    passages = rows * reps * loops
    coef = 32.0 * (2 * width) / math.sqrt(passages)
    dup = max(1, reps * LANES // width)
    t_own = teacher.shape[1] // (reps * PIECE)
    pieces = 1 + 2 * t_own
    strips = width // LANES
    steps = strips * pieces
    total = rows * reps
    f32, bf16 = jnp.float32, jnp.bfloat16
    dma = pltpu.SemaphoreType.DMA
    flops = 4 * total * pieces * PIECE * width
    return pl.pallas_call(
        functools.partial(kernel, loops, reps, coef, dup),
        out_shape=jax.ShapeDtypeStruct((rows, width), f32),
        in_specs=[pl.BlockSpec(memory_space=pltpu.HBM)] * 2,
        out_specs=pl.BlockSpec(memory_space=pltpu.VMEM),
        scratch_shapes=[
            pltpu.VMEM((rows, width), bf16),
            pltpu.VMEM((rows, teacher.shape[1]), bf16),
            pltpu.VMEM((rows, LANES), f32),
            pltpu.VMEM((rows, LANES), f32),
            pltpu.VMEM((rows, LANES), f32),
            pltpu.VMEM((total, width), bf16),
            pltpu.VMEM((strips, LANES, total), bf16),
            pltpu.VMEM((pieces, total, PIECE), bf16),
            pltpu.VMEM((reps, t_own, rows, PIECE), bf16),
            pltpu.VMEM((steps, LANES, PIECE), f32),
            pltpu.VMEM((steps, LANES, PIECE), bf16),
            pltpu.VMEM((steps, LANES, PIECE), bf16),
            pltpu.VMEM((steps, LANES, PIECE), bf16),
            pltpu.VMEM((steps, LANES, PIECE), bf16),
            pltpu.VMEM((strips, pieces, LANES, PIECE), bf16),
            pltpu.VMEM((strips, reps, rows, LANES), bf16),
            pltpu.VMEM((strips, reps, rows, LANES), bf16),
            pltpu.VMEM((strips, rows, LANES), f32),
            pltpu.VMEM((rows, LANES), f32),
            pltpu.VMEM((rows, LANES), f32),
            dma((2,)),
            dma((2,)),
            dma((strips, reps)),
            dma((strips, reps)),
            dma((t_own, reps)),
            dma((t_own, reps)),
            dma((t_own + 1, reps)),
            dma((t_own + 1, reps)),
            dma((steps,)),
            dma((steps,)),
            dma((steps,)),
            dma((steps,)),
            dma((strips, reps)),
            dma((strips, reps)),
            dma((2,)),
        ],
        compiler_params=pltpu.CompilerParams(
            collective_id=0, has_side_effects=True, vmem_limit_bytes=48 * 1024 * 1024
        ),
        cost_estimate=pl.CostEstimate(flops=flops, bytes_accessed=4 * rows * width, transcendentals=0),
    )(student, teacher)


def solution(mesh):
    placed = P(("loop", "rep"), "sec")
    return jax.shard_map(
        functools.partial(body, mesh.shape["loop"], mesh.shape["rep"]),
        mesh=mesh, in_specs=(placed, placed), out_specs=placed, check_vma=False,
    )
```

```python
import functools
import math

import jax
import jax.numpy as jnp
from jax import lax
from jax.experimental import pallas as pl
from jax.experimental.pallas import tpu as pltpu
from jax.sharding import PartitionSpec as P

MESH = pl.DeviceIdType.MESH
LANES = 128
PIECE = 256
LAG = 3
IDLE = 3
EPS = 1e-6


def kernel(
    loops, reps, coef, dup, s_hbm, t_hbm, out_ref,
    s_ref, t_ref, stat_tx, stat_rx, inv_keep, cols_all, cols_t, feats, feats_tx, own, right_tx, left_tx,
    from_left, from_right, full, part_tx, part_rx, part_own, inner_tx, inner_rx,
    load_sem, stat_sem, strip_send, strip_recv, gather_send, gather_recv, swap_send, swap_recv,
    right_send, right_recv, left_send, left_recv, part_send, part_recv, inner_sem,
):
    z = lax.axis_index("loop")
    b = lax.axis_index("rep")
    c = lax.axis_index("sec")
    rows, width = s_ref.shape
    pieces, total_rows, _ = feats.shape
    t_own = (pieces - 1) // 2
    strips = width // LANES
    steps = strips * pieces
    early = 2 * strips
    later = pieces - 2
    sibling = (z, b, 1 - c)
    has_left = z > 0
    has_right = z < loops - 1

    def peer(d):
        return lax.rem(b + d, reps)

    def span(q):
        return pl.ds(pl.multiple_of(q * rows, rows), rows)

    def lanes(j):
        return pl.ds(pl.multiple_of(j * LANES, LANES), LANES)

    load_s = pltpu.make_async_copy(s_hbm, s_ref, load_sem.at[0])
    load_t = pltpu.make_async_copy(t_hbm, t_ref, load_sem.at[1])
    load_s.start()
    load_t.start()
    barrier = pltpu.get_barrier_semaphore()
    for d in range(1, reps):
        pl.semaphore_signal(barrier, inc=1, device_id=(z, peer(d), c), device_id_type=MESH)
    pl.semaphore_signal(barrier, inc=1, device_id=sibling, device_id_type=MESH)

    @pl.when(has_left)
    def _():
        pl.semaphore_signal(barrier, inc=1, device_id=(z - 1, b, c), device_id_type=MESH)

    @pl.when(has_right)
    def _():
        pl.semaphore_signal(barrier, inc=1, device_id=(z + 1, b, c), device_id_type=MESH)

    load_s.wait()
    s32 = s_ref[...].astype(jnp.float32)
    part_s = jnp.sum(s32 * s32, axis=1, keepdims=True)
    load_t.wait()
    t32 = t_ref[...].astype(jnp.float32)
    part_t = jnp.sum(t32 * t32, axis=1, keepdims=True)
    lane = lax.broadcasted_iota(jnp.int32, (rows, LANES), 1)
    stat_tx[...] = jnp.where(lane < LANES // 2, part_s, part_t)

    pl.semaphore_wait(barrier, reps + has_left.astype(jnp.int32) + has_right.astype(jnp.int32))

    def remote(src, dst, send, recv, device):
        return pltpu.make_async_remote_copy(
            src_ref=src, dst_ref=dst, send_sem=send, recv_sem=recv,
            device_id=device, device_id_type=MESH,
        )

    stat = remote(stat_tx, stat_rx, stat_sem.at[0], stat_sem.at[1], sibling)
    stat.start()
    stat.wait()
    inv = lax.rsqrt(stat_tx[...] + stat_rx[...] + EPS)
    inv_s = inv[:, :1]
    inv_t = inv[:, LANES - 1:]
    inv_keep[...] = jnp.broadcast_to(inv_s, (rows, LANES))
    mine = span(b)
    cols_all[mine, :] = (s_ref[...].astype(jnp.float32) * inv_s).astype(jnp.bfloat16)

    def strip_to(d, j):
        at = lanes(j)
        return remote(cols_all.at[mine, at], cols_all.at[mine, at],
                      strip_send.at[j, d], strip_recv.at[j, d], (z, peer(d), c))

    def piece_to(d, p):
        return remote(feats_tx.at[peer(d), p], feats.at[2 * p, mine],
                      gather_send.at[p, d], gather_recv.at[p, d], (z, peer(d), c))

    def send_strip(j):
        if j < strips:
            for d in range(1, reps):
                strip_to(d, j).start()

    def send_piece(p):
        for d in range(1, reps):
            piece_to(d, p).start()

    send_strip(0)
    for p in range(t_own):
        for q in range(reps):
            lo = (q * t_own + p) * PIECE
            feats_tx[q, p] = (t_ref[:, lo:lo + PIECE].astype(jnp.float32) * inv_t).astype(jnp.bfloat16)
        if p == 0:
            send_piece(0)
            send_strip(1)
        feats[2 * p, mine, :] = feats_tx[b, p]

    block = b // dup

    def came(d):
        return span(lax.rem(b - d + reps, reps))

    def piece_over(d, p):
        at = came(d)
        return remote(feats.at[2 * p, at], feats.at[2 * p + 1, at],
                      swap_send.at[p, d], swap_recv.at[p, d], sibling)

    def block_over(d):
        at = came(d)
        return remote(cols_all.at[at, lanes(block)], feats.at[pieces - 1, at, pl.ds(LANES, LANES)],
                      swap_send.at[t_own, d], swap_recv.at[t_own, d], sibling)

    def strip_in(j):
        for d in range(1, reps):
            strip_to(d, j).wait_recv()

    def turn(j):
        cols_t[j] = cols_all[:, j * LANES:(j + 1) * LANES].T

    def rightward(k):
        return remote(right_tx.at[k], from_left.at[k], right_send.at[k], right_recv.at[k], (z + 1, b, c))

    def leftward(k):
        return remote(left_tx.at[k], from_right.at[k], left_send.at[k], left_recv.at[k], (z - 1, b, c))

    def result(j, d):
        return remote(part_tx.at[j, peer(d)], part_rx.at[j, d],
                      part_send.at[j, d], part_recv.at[j, d], (z, peer(d), c))

    def strip_and_piece(k):
        first = k < early
        j = jnp.where(first, k // 2, (k - early) // later)
        p = jnp.where(first, lax.rem(k, 2), 2 + lax.rem(k - early + later * strips, later))
        return j, p

    def produce(k):
        j, p = strip_and_piece(k)
        own[k] = jnp.dot(cols_t[j], feats[p], preferred_element_type=jnp.float32)

    def up(k):
        @pl.when(has_left)
        def _():
            rightward(k).wait_recv()

        @pl.when(has_right)
        def _():
            @pl.when(has_left)
            def _():
                right_tx[k] = (own[k] + from_left[k].astype(jnp.float32)).astype(jnp.bfloat16)

            @pl.when(jnp.logical_not(has_left))
            def _():
                right_tx[k] = own[k].astype(jnp.bfloat16)
            rightward(k).start()

    def down(k):
        @pl.when(has_right)
        def _():
            leftward(k).wait_recv()

        @pl.when(has_left)
        def _():
            @pl.when(has_right)
            def _():
                left_tx[k] = (own[k] + from_right[k].astype(jnp.float32)).astype(jnp.bfloat16)

            @pl.when(jnp.logical_not(has_right))
            def _():
                left_tx[k] = own[k].astype(jnp.bfloat16)
            leftward(k).start()

    def across(left, right):
        return lax.dot_general(left, right, (((1,), (1,)), ((), ())), preferred_element_type=jnp.float32)

    def finish(k):
        j, p = strip_and_piece(k)

        last = p == pieces - 1
        sign = jnp.where(last, 1.0 / dup, -1.0)

        @pl.when(jnp.logical_and(has_left, has_right))
        def _():
            total = own[k] + from_left[k].astype(jnp.float32) + from_right[k].astype(jnp.float32)
            full[j, p] = (total * sign).astype(jnp.bfloat16)

        @pl.when(jnp.logical_not(has_left))
        def _():
            full[j, p] = ((own[k] + from_right[k].astype(jnp.float32)) * sign).astype(jnp.bfloat16)

        @pl.when(jnp.logical_not(has_right))
        def _():
            full[j, p] = ((own[k] + from_left[k].astype(jnp.float32)) * sign).astype(jnp.bfloat16)

        @pl.when(last)
        def _():
            total = across(
                jnp.concatenate([feats[q] for q in range(pieces)], axis=1),
                jnp.concatenate([full[j, q] for q in range(pieces)], axis=1),
            )
            for q in range(reps):
                part_tx[j, q] = total[q * rows:(q + 1) * rows].astype(jnp.bfloat16)

                @pl.when(b == q)
                def _():
                    part_own[j] = total[q * rows:(q + 1) * rows]
            for d in range(1, reps):
                result(j, d).start()

    lag_up = LAG * z
    lag_down = LAG * (loops - 1 - z)
    lag_end = jnp.maximum(lag_up, lag_down)

    def chunk_at(i):
        k = jnp.where(i < early, i, i - IDLE)
        idle = jnp.logical_and(i >= early, i < early + IDLE)
        return k, jnp.logical_and(jnp.logical_not(idle), jnp.logical_and(i >= 0, k < steps))

    def tick(i, carry):
        def serve(lag, act, when=True):
            k, live = chunk_at(i - lag)

            @pl.when(jnp.logical_and(live, when))
            def _():
                act(k)

        lower = lag_down > lag_up
        serve(lag_down, down, lower)
        serve(lag_up, up)
        serve(lag_down, down, jnp.logical_not(lower))
        serve(lag_end, finish)
        return carry

    def make(k, carry):
        produce(k)
        return tick(jnp.where(k < early, k, k + IDLE), carry)

    def pieces_in(p):
        for d in range(1, reps):
            piece_to(d, p).wait_recv()
            piece_over(d, p).start()

    for p in range(t_own):
        piece_over(0, p).start()
    block_over(0).start()
    strip_in(0)
    turn(0)
    pieces_in(0)
    send_strip(2)
    make(0, 0)
    for d in range(reps):
        piece_over(d, 0).wait_recv()
    make(1, 0)
    for j in range(1, strips):
        strip_in(j)
        send_strip(j + 2)
        if j == min(2, strips - 1):
            for p in range(1, t_own):
                send_piece(p)
        turn(j)
        lax.fori_loop(2 * j, 2 * j + 2, make, 0)
    for d in range(1, reps):
        block_over(d).start()
    feats[pieces - 1, :, :LANES] = cols_all[:, lanes(block)]
    lax.fori_loop(early, early + IDLE, tick, 0)
    for p in range(1, t_own):
        pieces_in(p)
    for d in range(reps):
        for p in range(1, t_own):
            piece_over(d, p).wait_recv()
        block_over(d).wait_recv()
    lax.fori_loop(early, steps, make, 0)
    lax.fori_loop(steps + IDLE, steps + IDLE + LAG * (loops - 1), tick, 0)

    norm = cols_all[mine, :].astype(jnp.float32)
    inner = jnp.zeros((rows, 1), jnp.float32)
    grads = []
    for j in range(strips):
        grad = part_own[j]
        for d in range(1, reps):
            result(j, d).wait_recv()
            grad = grad + part_rx[j, d].astype(jnp.float32)
        grad = grad * coef
        grads.append(grad)
        inner = inner + jnp.sum(grad * norm[:, j * LANES:(j + 1) * LANES], axis=1, keepdims=True)
    inner_tx[...] = jnp.broadcast_to(inner, (rows, LANES))
    swap = remote(inner_tx, inner_rx, inner_sem.at[0], inner_sem.at[1], sibling)
    swap.start()
    for d in range(reps):
        for p in range(t_own):
            piece_over(d, p).wait_send()
            if d:
                piece_to(d, p).wait_send()
        block_over(d).wait_send()
    for j in range(strips):
        for d in range(1, reps):
            strip_to(d, j).wait_send()
            result(j, d).wait_send()

    def drain(k, carry):
        @pl.when(has_right)
        def _():
            rightward(k).wait_send()

        @pl.when(has_left)
        def _():
            leftward(k).wait_send()
        return carry

    lax.fori_loop(0, steps, drain, 0)

    swap.wait_recv()
    inner_all = inner_tx[...] + inner_rx[...]
    for j in range(strips):
        at = slice(j * LANES, (j + 1) * LANES)
        out_ref[:, at] = (grads[j] - inner_all * norm[:, at]) * inv_keep[...]

    swap.wait_send()


def body(loops, reps, student, teacher):
    rows, width = student.shape
    passages = rows * reps * loops
    coef = 32.0 * (2 * width) / math.sqrt(passages)
    dup = max(1, reps * LANES // width)
    t_own = teacher.shape[1] // (reps * PIECE)
    pieces = 1 + 2 * t_own
    strips = width // LANES
    steps = strips * pieces
    total = rows * reps
    f32, bf16 = jnp.float32, jnp.bfloat16
    dma = pltpu.SemaphoreType.DMA
    flops = 4 * total * pieces * PIECE * width
    return pl.pallas_call(
        functools.partial(kernel, loops, reps, coef, dup),
        out_shape=jax.ShapeDtypeStruct((rows, width), f32),
        in_specs=[pl.BlockSpec(memory_space=pltpu.HBM)] * 2,
        out_specs=pl.BlockSpec(memory_space=pltpu.VMEM),
        scratch_shapes=[
            pltpu.VMEM((rows, width), bf16),
            pltpu.VMEM((rows, teacher.shape[1]), bf16),
            pltpu.VMEM((rows, LANES), f32),
            pltpu.VMEM((rows, LANES), f32),
            pltpu.VMEM((rows, LANES), f32),
            pltpu.VMEM((total, width), bf16),
            pltpu.VMEM((strips, LANES, total), bf16),
            pltpu.VMEM((pieces, total, PIECE), bf16),
            pltpu.VMEM((reps, t_own, rows, PIECE), bf16),
            pltpu.VMEM((steps, LANES, PIECE), f32),
            pltpu.VMEM((steps, LANES, PIECE), bf16),
            pltpu.VMEM((steps, LANES, PIECE), bf16),
            pltpu.VMEM((steps, LANES, PIECE), bf16),
            pltpu.VMEM((steps, LANES, PIECE), bf16),
            pltpu.VMEM((strips, pieces, LANES, PIECE), bf16),
            pltpu.VMEM((strips, reps, rows, LANES), bf16),
            pltpu.VMEM((strips, reps, rows, LANES), bf16),
            pltpu.VMEM((strips, rows, LANES), f32),
            pltpu.VMEM((rows, LANES), f32),
            pltpu.VMEM((rows, LANES), f32),
            dma((2,)),
            dma((2,)),
            dma((strips, reps)),
            dma((strips, reps)),
            dma((t_own, reps)),
            dma((t_own, reps)),
            dma((t_own + 1, reps)),
            dma((t_own + 1, reps)),
            dma((steps,)),
            dma((steps,)),
            dma((steps,)),
            dma((steps,)),
            dma((strips, reps)),
            dma((strips, reps)),
            dma((2,)),
        ],
        compiler_params=pltpu.CompilerParams(
            collective_id=0, has_side_effects=True, vmem_limit_bytes=48 * 1024 * 1024
        ),
        cost_estimate=pl.CostEstimate(flops=flops, bytes_accessed=4 * rows * width, transcendentals=0),
    )(student, teacher)


def solution(mesh):
    placed = P(("loop", "rep"), "sec")
    return jax.shard_map(
        functools.partial(body, mesh.shape["loop"], mesh.shape["rep"]),
        mesh=mesh, in_specs=(placed, placed), out_specs=placed, check_vma=False,
    )
```

```python
import functools
import math

import jax
import jax.numpy as jnp
from jax import lax
from jax.experimental import pallas as pl
from jax.experimental.pallas import tpu as pltpu
from jax.sharding import PartitionSpec as P

MESH = pl.DeviceIdType.MESH
LANES = 128
PIECE = 256
LAG = 3
IDLE = 3
EPS = 1e-6


def kernel(
    loops, reps, coef, dup, s_hbm, t_hbm, out_ref,
    s_ref, t_ref, stat_tx, stat_rx, inv_keep, cols_all, cols_t, feats, feats_tx, own, right_tx, left_tx,
    from_left, from_right, full, part_tx, part_rx, part_own, inner_tx, inner_rx,
    load_sem, stat_sem, strip_send, strip_recv, gather_send, gather_recv, swap_send, swap_recv,
    right_send, right_recv, left_send, left_recv, part_send, part_recv, inner_sem,
):
    z = lax.axis_index("loop")
    b = lax.axis_index("rep")
    c = lax.axis_index("sec")
    rows, width = s_ref.shape
    pieces, total_rows, _ = feats.shape
    t_own = (pieces - 1) // 2
    strips = width // LANES
    steps = strips * pieces
    early = 2 * strips
    later = pieces - 2
    sibling = (z, b, 1 - c)
    has_left = z > 0
    has_right = z < loops - 1

    def peer(d):
        return lax.rem(b + d, reps)

    def span(q):
        return pl.ds(pl.multiple_of(q * rows, rows), rows)

    def lanes(j):
        return pl.ds(pl.multiple_of(j * LANES, LANES), LANES)

    load_s = pltpu.make_async_copy(s_hbm, s_ref, load_sem.at[0])
    load_t = pltpu.make_async_copy(t_hbm, t_ref, load_sem.at[1])
    load_s.start()
    load_t.start()
    barrier = pltpu.get_barrier_semaphore()
    for d in range(1, reps):
        pl.semaphore_signal(barrier, inc=1, device_id=(z, peer(d), c), device_id_type=MESH)
    pl.semaphore_signal(barrier, inc=1, device_id=sibling, device_id_type=MESH)

    @pl.when(has_left)
    def _():
        pl.semaphore_signal(barrier, inc=1, device_id=(z - 1, b, c), device_id_type=MESH)

    @pl.when(has_right)
    def _():
        pl.semaphore_signal(barrier, inc=1, device_id=(z + 1, b, c), device_id_type=MESH)

    load_s.wait()
    s32 = s_ref[...].astype(jnp.float32)
    part_s = jnp.sum(s32 * s32, axis=1, keepdims=True)
    load_t.wait()
    t32 = t_ref[...].astype(jnp.float32)
    part_t = jnp.sum(t32 * t32, axis=1, keepdims=True)
    lane = lax.broadcasted_iota(jnp.int32, (rows, LANES), 1)
    stat_tx[...] = jnp.where(lane < LANES // 2, part_s, part_t)

    pl.semaphore_wait(barrier, reps + has_left.astype(jnp.int32) + has_right.astype(jnp.int32))

    def remote(src, dst, send, recv, device):
        return pltpu.make_async_remote_copy(
            src_ref=src, dst_ref=dst, send_sem=send, recv_sem=recv,
            device_id=device, device_id_type=MESH,
        )

    stat = remote(stat_tx, stat_rx, stat_sem.at[0], stat_sem.at[1], sibling)
    stat.start()
    stat.wait()
    inv = lax.rsqrt(stat_tx[...] + stat_rx[...] + EPS)
    inv_s = inv[:, :1]
    inv_t = inv[:, LANES - 1:]
    inv_keep[...] = jnp.broadcast_to(inv_s, (rows, LANES))
    mine = span(b)
    cols_all[mine, :] = (s_ref[...].astype(jnp.float32) * inv_s).astype(jnp.bfloat16)

    def strip_to(d, j):
        at = lanes(j)
        return remote(cols_all.at[mine, at], cols_all.at[mine, at],
                      strip_send.at[j, d], strip_recv.at[j, d], (z, peer(d), c))

    def piece_to(d, p):
        return remote(feats_tx.at[peer(d), p], feats.at[2 * p, mine],
                      gather_send.at[p, d], gather_recv.at[p, d], (z, peer(d), c))

    def send_strip(j):
        if j < strips:
            for d in range(1, reps):
                strip_to(d, j).start()

    def send_piece(p):
        for d in range(1, reps):
            piece_to(d, p).start()

    send_strip(0)
    for p in range(t_own):
        for q in range(reps):
            lo = (q * t_own + p) * PIECE
            feats_tx[q, p] = (t_ref[:, lo:lo + PIECE].astype(jnp.float32) * inv_t).astype(jnp.bfloat16)
        if p == 0:
            send_piece(0)
            send_strip(1)
        feats[2 * p, mine, :] = feats_tx[b, p]

    block = b // dup

    def came(d):
        return span(lax.rem(b - d + reps, reps))

    def piece_over(d, p):
        at = came(d)
        return remote(feats.at[2 * p, at], feats.at[2 * p + 1, at],
                      swap_send.at[p, d], swap_recv.at[p, d], sibling)

    def block_over(d):
        at = came(d)
        return remote(cols_all.at[at, lanes(block)], feats.at[pieces - 1, at, pl.ds(LANES, LANES)],
                      swap_send.at[t_own, d], swap_recv.at[t_own, d], sibling)

    def strip_in(j):
        for d in range(1, reps):
            strip_to(d, j).wait_recv()

    def turn(j):
        cols_t[j] = cols_all[:, j * LANES:(j + 1) * LANES].T

    def rightward(k):
        return remote(right_tx.at[k], from_left.at[k], right_send.at[k], right_recv.at[k], (z + 1, b, c))

    def leftward(k):
        return remote(left_tx.at[k], from_right.at[k], left_send.at[k], left_recv.at[k], (z - 1, b, c))

    def result(j, d):
        return remote(part_tx.at[j, peer(d)], part_rx.at[j, d],
                      part_send.at[j, d], part_recv.at[j, d], (z, peer(d), c))

    def strip_and_piece(k):
        first = k < early
        j = jnp.where(first, k // 2, (k - early) // later)
        p = jnp.where(first, lax.rem(k, 2), 2 + lax.rem(k - early + later * strips, later))
        return j, p

    def produce(k):
        j, p = strip_and_piece(k)
        own[k] = jnp.dot(cols_t[j], feats[p], preferred_element_type=jnp.float32)

    def up(k):
        @pl.when(has_left)
        def _():
            rightward(k).wait_recv()

        @pl.when(has_right)
        def _():
            @pl.when(has_left)
            def _():
                right_tx[k] = (own[k] + from_left[k].astype(jnp.float32)).astype(jnp.bfloat16)

            @pl.when(jnp.logical_not(has_left))
            def _():
                right_tx[k] = own[k].astype(jnp.bfloat16)
            rightward(k).start()

    def down(k):
        @pl.when(has_right)
        def _():
            leftward(k).wait_recv()

        @pl.when(has_left)
        def _():
            @pl.when(has_right)
            def _():
                left_tx[k] = (own[k] + from_right[k].astype(jnp.float32)).astype(jnp.bfloat16)

            @pl.when(jnp.logical_not(has_right))
            def _():
                left_tx[k] = own[k].astype(jnp.bfloat16)
            leftward(k).start()

    def across(left, right):
        return lax.dot_general(left, right, (((1,), (1,)), ((), ())), preferred_element_type=jnp.float32)

    def finish(k):
        j, p = strip_and_piece(k)

        last = p == pieces - 1
        sign = jnp.where(last, 1.0 / dup, -1.0)

        @pl.when(jnp.logical_and(has_left, has_right))
        def _():
            total = own[k] + from_left[k].astype(jnp.float32) + from_right[k].astype(jnp.float32)
            full[j, p] = (total * sign).astype(jnp.bfloat16)

        @pl.when(jnp.logical_not(has_left))
        def _():
            full[j, p] = ((own[k] + from_right[k].astype(jnp.float32)) * sign).astype(jnp.bfloat16)

        @pl.when(jnp.logical_not(has_right))
        def _():
            full[j, p] = ((own[k] + from_left[k].astype(jnp.float32)) * sign).astype(jnp.bfloat16)

        @pl.when(last)
        def _():
            total = across(
                jnp.concatenate([feats[q] for q in range(pieces)], axis=1),
                jnp.concatenate([full[j, q] for q in range(pieces)], axis=1),
            )
            for q in range(reps):
                part_tx[j, q] = total[q * rows:(q + 1) * rows].astype(jnp.bfloat16)

                @pl.when(b == q)
                def _():
                    part_own[j] = total[q * rows:(q + 1) * rows]
            for d in range(1, reps):
                result(j, d).start()

    lag_up = LAG * z
    lag_down = LAG * (loops - 1 - z)
    lag_end = jnp.maximum(lag_up, lag_down)

    def chunk_at(i):
        k = jnp.where(i < early, i, i - IDLE)
        idle = jnp.logical_and(i >= early, i < early + IDLE)
        return k, jnp.logical_and(jnp.logical_not(idle), jnp.logical_and(i >= 0, k < steps))

    def tick(i, carry):
        def serve(lag, act, when=True):
            k, live = chunk_at(i - lag)

            @pl.when(jnp.logical_and(live, when))
            def _():
                act(k)

        lower = lag_down > lag_up
        serve(lag_down, down, lower)
        serve(lag_up, up)
        serve(lag_down, down, jnp.logical_not(lower))
        serve(lag_end, finish)
        return carry

    def make(k, carry):
        produce(k)
        return tick(jnp.where(k < early, k, k + IDLE), carry)

    def pieces_in(p):
        for d in range(1, reps):
            piece_to(d, p).wait_recv()
            piece_over(d, p).start()

    for p in range(t_own):
        piece_over(0, p).start()
    block_over(0).start()
    strip_in(0)
    turn(0)
    pieces_in(0)
    for j in range(2, strips):
        send_strip(j)
    make(0, 0)
    for d in range(reps):
        piece_over(d, 0).wait_recv()
    make(1, 0)
    for j in range(1, strips):
        strip_in(j)
        if j == 1:
            for p in range(1, t_own):
                send_piece(p)
        turn(j)
        lax.fori_loop(2 * j, 2 * j + 2, make, 0)
    for d in range(1, reps):
        block_over(d).start()
    feats[pieces - 1, :, :LANES] = cols_all[:, lanes(block)]
    lax.fori_loop(early, early + IDLE, tick, 0)
    for p in range(1, t_own):
        pieces_in(p)
    for d in range(reps):
        for p in range(1, t_own):
            piece_over(d, p).wait_recv()
        block_over(d).wait_recv()
    lax.fori_loop(early, steps, make, 0)
    lax.fori_loop(steps + IDLE, steps + IDLE + LAG * (loops - 1), tick, 0)

    norm = cols_all[mine, :].astype(jnp.float32)
    inner = jnp.zeros((rows, 1), jnp.float32)
    grads = []
    for j in range(strips):
        grad = part_own[j]
        for d in range(1, reps):
            result(j, d).wait_recv()
            grad = grad + part_rx[j, d].astype(jnp.float32)
        grad = grad * coef
        grads.append(grad)
        inner = inner + jnp.sum(grad * norm[:, j * LANES:(j + 1) * LANES], axis=1, keepdims=True)
    inner_tx[...] = jnp.broadcast_to(inner, (rows, LANES))
    swap = remote(inner_tx, inner_rx, inner_sem.at[0], inner_sem.at[1], sibling)
    swap.start()
    for d in range(reps):
        for p in range(t_own):
            piece_over(d, p).wait_send()
            if d:
                piece_to(d, p).wait_send()
        block_over(d).wait_send()
    for j in range(strips):
        for d in range(1, reps):
            strip_to(d, j).wait_send()
            result(j, d).wait_send()

    def drain(k, carry):
        @pl.when(has_right)
        def _():
            rightward(k).wait_send()

        @pl.when(has_left)
        def _():
            leftward(k).wait_send()
        return carry

    lax.fori_loop(0, steps, drain, 0)

    swap.wait_recv()
    inner_all = inner_tx[...] + inner_rx[...]
    for j in range(strips):
        at = slice(j * LANES, (j + 1) * LANES)
        out_ref[:, at] = (grads[j] - inner_all * norm[:, at]) * inv_keep[...]

    swap.wait_send()


def body(loops, reps, student, teacher):
    rows, width = student.shape
    passages = rows * reps * loops
    coef = 32.0 * (2 * width) / math.sqrt(passages)
    dup = max(1, reps * LANES // width)
    t_own = teacher.shape[1] // (reps * PIECE)
    pieces = 1 + 2 * t_own
    strips = width // LANES
    steps = strips * pieces
    total = rows * reps
    f32, bf16 = jnp.float32, jnp.bfloat16
    dma = pltpu.SemaphoreType.DMA
    flops = 4 * total * pieces * PIECE * width
    return pl.pallas_call(
        functools.partial(kernel, loops, reps, coef, dup),
        out_shape=jax.ShapeDtypeStruct((rows, width), f32),
        in_specs=[pl.BlockSpec(memory_space=pltpu.HBM)] * 2,
        out_specs=pl.BlockSpec(memory_space=pltpu.VMEM),
        scratch_shapes=[
            pltpu.VMEM((rows, width), bf16),
            pltpu.VMEM((rows, teacher.shape[1]), bf16),
            pltpu.VMEM((rows, LANES), f32),
            pltpu.VMEM((rows, LANES), f32),
            pltpu.VMEM((rows, LANES), f32),
            pltpu.VMEM((total, width), bf16),
            pltpu.VMEM((strips, LANES, total), bf16),
            pltpu.VMEM((pieces, total, PIECE), bf16),
            pltpu.VMEM((reps, t_own, rows, PIECE), bf16),
            pltpu.VMEM((steps, LANES, PIECE), f32),
            pltpu.VMEM((steps, LANES, PIECE), bf16),
            pltpu.VMEM((steps, LANES, PIECE), bf16),
            pltpu.VMEM((steps, LANES, PIECE), bf16),
            pltpu.VMEM((steps, LANES, PIECE), bf16),
            pltpu.VMEM((strips, pieces, LANES, PIECE), bf16),
            pltpu.VMEM((strips, reps, rows, LANES), bf16),
            pltpu.VMEM((strips, reps, rows, LANES), bf16),
            pltpu.VMEM((strips, rows, LANES), f32),
            pltpu.VMEM((rows, LANES), f32),
            pltpu.VMEM((rows, LANES), f32),
            dma((2,)),
            dma((2,)),
            dma((strips, reps)),
            dma((strips, reps)),
            dma((t_own, reps)),
            dma((t_own, reps)),
            dma((t_own + 1, reps)),
            dma((t_own + 1, reps)),
            dma((steps,)),
            dma((steps,)),
            dma((steps,)),
            dma((steps,)),
            dma((strips, reps)),
            dma((strips, reps)),
            dma((2,)),
        ],
        compiler_params=pltpu.CompilerParams(
            collective_id=0, has_side_effects=True, vmem_limit_bytes=48 * 1024 * 1024
        ),
        cost_estimate=pl.CostEstimate(flops=flops, bytes_accessed=4 * rows * width, transcendentals=0),
    )(student, teacher)


def solution(mesh):
    placed = P(("loop", "rep"), "sec")
    return jax.shard_map(
        functools.partial(body, mesh.shape["loop"], mesh.shape["rep"]),
        mesh=mesh, in_specs=(placed, placed), out_specs=placed, check_vma=False,
    )
```
